256 devices in a mesh: dp: 8 (over z_lo, y), tensor: 32 (over x, z_hi, core).
Axes of the slice: x: 4, y: 4, z: 8 (z_hi: 4, z_lo: 2; z = z_hi * 2 + z_lo), core: 2. Of those that a mesh axis runs over, the one named last changes fastest.
Arguments:
- tokens: bfloat16 [1024, 8192], P('dp', 'tensor'), may hold values from -20 to 20
- out_grads: bfloat16 [1024, 16384], P('dp', 'tensor'), may hold values from -20 to 20
- basis_act: bfloat16 [8192, 8192], P('dp', 'tensor'), may hold values from -0.0625 to 0.0625
- basis_grad: bfloat16 [16384, 16384], P('dp', 'tensor'), may hold values from -0.046875 to 0.046875
Outputs:
- cov_act: float32 [8192, 8192], P('tensor', 'dp')
- cov_grad: float32 [16384, 16384], P('tensor', 'dp')
- correction: float32 [8192, 16384], P('dp', 'tensor')
The draws below stay inside these ranges and needn't reach their ends.
All inputs are finite; a program needn't handle non-finite values.
Results may differ from the reference program's by a relative error of at most 0.0009.
Values may be sent and summed in bfloat16 or wider, within the bound.
No kernel may reach another device: no remote copies, remote signals or barrier semaphores. Data moves between devices by JAX's collectives and lax.ppermute only.
A program may use at most 64 MiB of HBM per device.

```python
import jax
import jax.numpy as jnp

D = 8192
FFW = 16384
TOKENS = 1024


def scaled_field(key, rows, cols):
    keys = jax.random.split(key, 5)
    normal = jnp.clip(jax.random.normal(keys[0], (rows, cols), jnp.float32), -4.0, 4.0)
    base = normal
    row_scale = 10.0 ** jax.random.uniform(keys[3], (rows, 1), jnp.float32)
    col_scale = 10.0 ** jax.random.uniform(keys[4], (1, cols), jnp.float32, minval=-0.5, maxval=0.5)
    return (0.15 * base * row_scale * col_scale).astype(jnp.bfloat16)


def draw_tokens(key, part):
    key = jax.random.fold_in(key, 11)
    return scaled_field(key, TOKENS, D)


def draw_out_grads(key, part):
    key = jax.random.fold_in(key, 12)
    return scaled_field(key, TOKENS, FFW)


def shard_levels(key, dims, shards, low, high):
    def one(dim, shards_of):
        heights = jax.random.uniform(jax.random.fold_in(jax.random.fold_in(key, 6), dim), (shards_of,), jnp.float32, low / len(shards), high / len(shards))
        return jnp.repeat(jnp.exp(heights), dims[dim] // shards_of).reshape((-1,) + (1,) * (len(dims) - dim - 1))

    level = one(*shards[0])
    for cut in shards[1:]:
        level = level * one(*cut)
    return level


def normal_values(rng, shape, width, bound, pieces=(), held_as=jnp.bfloat16):
    drawn = jax.random.normal(rng, shape, jnp.float32) * width
    if len(pieces) > 0:
        drawn = shard_levels(rng, shape, pieces, -0.22, 0.18) * drawn
    return jnp.clip(drawn, min=-bound, max=bound).astype(held_as)


def setup_inputs(seed: int = 0) -> dict:
    streams_of = jax.random.split(jax.random.key(seed), 5)
    return {
        "tokens": draw_tokens(jax.random.fold_in(streams_of[4], 71), 0),
        "out_grads": draw_out_grads(jax.random.fold_in(streams_of[4], 71), 0),
        "basis_act": normal_values(streams_of[2], (D, D), D ** -0.5, 0.0625, ((0, 8), (1, 32))),
        "basis_grad": normal_values(streams_of[3], (FFW, FFW), FFW ** -0.5, 0.046875, ((0, 8), (1, 32))),
    }


def reference(tokens, out_grads, basis_act, basis_grad):
    cov_act = jnp.dot(tokens.T, tokens, preferred_element_type=jnp.float32) / TOKENS
    cov_grad = jnp.dot(out_grads.T, out_grads, preferred_element_type=jnp.float32) / TOKENS
    rot_act = jnp.dot(tokens, basis_act, preferred_element_type=jnp.float32)
    rot_grad = jnp.dot(out_grads, basis_grad, preferred_element_type=jnp.float32)
    sq_act = (rot_act * rot_act).astype(jnp.bfloat16)
    sq_grad = (rot_grad * rot_grad).astype(jnp.bfloat16)
    correction = jnp.dot(sq_act.T, sq_grad, preferred_element_type=jnp.float32) / TOKENS
    return cov_act, cov_grad, correction
```

```python
import itertools

import jax
import jax.numpy as jnp
from jax import lax
from jax.sharding import Mesh, PartitionSpec as P

AXES = ("zl", "y", "x", "zh", "c")
SIZES = (2, 4, 4, 4, 2)
ZL, Y, X, ZH, C = range(5)


def device_index(q):
    index = 0
    for size, value in zip(SIZES, q):
        index = index * size + value
    return index


def permutation(target):
    every = itertools.product(*(range(size) for size in SIZES))
    return [(device_index(q), device_index(target(*q))) for q in every]


def shifted(value, axis, step):
    def target(*q):
        q = list(q)
        q[axis] = (q[axis] + step) % SIZES[axis]
        return q

    return lax.ppermute(value, AXES, permutation(target))


def to_group(zl, y, x, zh, c):
    row = (x & 1) * 2 + (zh >> 1)
    flip = zl ^ (x >> 1)
    return x >> 1, row, x ^ y ^ row, ((zh >> 1) ^ flip) * 2 + ((zh & 1) ^ flip), c


def gather_group(block, where):
    zl, y, x, zh, c = where
    rows, k = block.shape
    block = lax.ppermute(block, AXES, permutation(to_group))
    x_source = zl * 2 + (y >> 1)
    near = jnp.zeros((2 * rows, 2 * k), block.dtype)
    for step in (0, 1, -1, 2):
        piece = block if step == 0 else shifted(block, ZH, step)
        slot = (zh - step) & 3
        flip = (slot >> 1) ^ (y & 1)
        near = lax.dynamic_update_slice(
            near, piece, ((flip ^ zl) * rows, ((slot & 1) ^ flip) * k)
        )
    panel = jnp.zeros((8 * rows, 2 * k), block.dtype)
    left = shifted(near, X, 1)
    right = shifted(near, X, -1)
    far_low = shifted(right[:, :k], X, -1)
    far_high = shifted(left[:, k:], X, 1)
    for step, column, piece in (
        (0, 0, near), (1, 0, left), (-1, 0, right), (2, 0, far_low), (2, k, far_high)
    ):
        slot = ((x - step) & 3) ^ x_source ^ y
        panel = lax.dynamic_update_slice(panel, piece, (slot * 2 * rows, column))
    other = shifted(panel, C, 1)
    first = jnp.where(c == 0, panel, other).reshape(8 * rows, 2, k)
    second = jnp.where(c == 0, other, panel).reshape(8 * rows, 2, k)
    return jnp.stack([first, second], axis=2)


def sum_over_dp(part, where):
    zl, y, x, zh, c = where
    n = part.shape[1]
    part = part.reshape(4, 2, -1, n)
    pieces = [lax.dynamic_index_in_dim(part, y, 0, False)]
    for step in (1, -1, 2):
        piece = lax.dynamic_index_in_dim(part, (y + step) & 3, 0, False)
        pieces.append(shifted(piece, Y, step))
    def half(which):
        return sum(lax.dynamic_index_in_dim(piece, which, 0, False) for piece in pieces)

    return half(zl) + shifted(half(1 - zl), ZL, 1)


def gather_dp(block, where):
    zl, y, x, zh, c = where
    rows, n = block.shape
    other = shifted(block, ZL, 1)
    pair = jnp.concatenate(
        [jnp.where(zl == 0, block, other), jnp.where(zl == 0, other, block)], axis=0
    )
    whole = jnp.zeros((8 * rows, n), block.dtype)
    for step in (0, 1, -1, 2):
        piece = pair if step == 0 else shifted(pair, Y, step)
        whole = lax.dynamic_update_slice(whole, piece, (((y - step) & 3) * 2 * rows, 0))
    return whole


def contract_rows(left, right):
    return lax.dot_general(
        left, right, (((0,), (0,)), ((), ())), preferred_element_type=jnp.float32
    )


def body(tokens, out_grads, basis_act, basis_grad):
    where = tuple(lax.axis_index(axis) for axis in AXES)
    rows_total = tokens.shape[0] * 8
    n_act = tokens.shape[1]
    mine = jnp.concatenate([tokens, out_grads], axis=1)
    panel = gather_group(mine, where)
    own = lax.all_gather(mine, ("y", "zl"), axis=0, tiled=True)
    act_panel = panel[..., :n_act].reshape(rows_total, -1)
    grad_panel = panel[..., n_act:].reshape(rows_total, -1)
    part_act = jnp.dot(act_panel, basis_act, preferred_element_type=jnp.float32)
    part_grad = jnp.dot(grad_panel, basis_grad, preferred_element_type=jnp.float32)
    rot_act = sum_over_dp(part_act, where)
    rot_grad = sum_over_dp(part_grad, where)
    sq_act = (rot_act * rot_act).astype(jnp.bfloat16)
    sq_grad = (rot_grad * rot_grad).astype(jnp.bfloat16)
    square_panel = gather_group(sq_act, where).reshape(rows_total, -1)
    square_own = gather_dp(sq_grad, where)
    cov_act = contract_rows(own[:, :n_act], act_panel) / rows_total
    cov_grad = contract_rows(own[:, n_act:], grad_panel) / rows_total
    correction = contract_rows(square_panel, square_own) / rows_total
    return (cov_act, cov_grad, correction)


def solution(mesh):
    fine = Mesh(mesh.devices.reshape(SIZES), AXES)
    dp, tensor = ("zl", "y"), ("x", "zh", "c")
    placed = P(dp, tensor)
    return jax.shard_map(
        body,
        mesh=fine,
        in_specs=(placed,) * 4,
        out_specs=(P(tensor, dp), P(tensor, dp), placed),
        check_vma=False,
    )
```

```python
import itertools

import jax
import jax.numpy as jnp
from jax import lax
from jax.experimental import pallas as pl
from jax.experimental.pallas import tpu as pltpu
from jax.sharding import Mesh, PartitionSpec as P

AXES = ("zl", "y", "x", "zh", "c")
SIZES = (2, 4, 4, 4, 2)
ZL, Y, X, ZH, C = range(5)
STEPS = (0, 1, -1, 2)
ANY = pl.BlockSpec(memory_space=pl.ANY)
SCALARS = pl.BlockSpec(memory_space=pltpu.SMEM)
PARAMS = pltpu.CompilerParams(vmem_limit_bytes=48 * 1024 * 1024)


def device_index(q):
    index = 0
    for size, value in zip(SIZES, q):
        index = index * size + value
    return index


def permutation(target):
    every = itertools.product(*(range(size) for size in SIZES))
    return [(device_index(q), device_index(target(*q))) for q in every]


def shifted(value, axis, step):
    def target(*q):
        q = list(q)
        q[axis] = (q[axis] + step) % SIZES[axis]
        return q

    return lax.ppermute(value, AXES, permutation(target))


def folded(value):
    def target(zl, y, x, zh, c):
        return zl, y, (x - 1 + 2 * c) % SIZES[X], zh, c

    return lax.ppermute(value, AXES, permutation(target))


def to_group(zl, y, x, zh, c):
    row = (x & 1) * 2 + (zh >> 1)
    flip = zl ^ (x >> 1)
    return x >> 1, row, x ^ y ^ row, ((zh >> 1) ^ flip) * 2 + ((zh & 1) ^ flip), c


def x_slot(where, step):
    return ((where[X] - step) & 3) ^ (where[ZL] * 2 + (where[Y] >> 1)) ^ where[Y]


def y_slot(where, step):
    return (where[Y] - step) & 3


def z_slot(where, step):
    slot = (where[ZH] - step) & 3
    flip = (slot >> 1) ^ (where[Y] & 1)
    return flip ^ where[ZL], (slot & 1) ^ flip


def near_kernel(turned, where, *refs):
    *pieces, near, sems = refs
    copies = []
    for i, (step, piece) in enumerate(zip(STEPS, pieces)):
        zl, h = z_slot(where, step)
        tokens = piece.shape[1 if turned else 0]
        span = pl.ds(pl.multiple_of(zl * tokens, tokens), tokens)
        target = near.at[h, :, span] if turned else near.at[h, span, :]
        copies.append(pltpu.make_async_copy(piece, target, sems.at[i]))
        copies[-1].start()
    for copy in copies:
        copy.wait()


def gather_group(block, where, turned):
    block = lax.ppermute(block, AXES, permutation(to_group))
    pieces = [block if step == 0 else shifted(block, ZH, step) for step in STEPS]
    rows, columns = block.shape
    shape = (2, rows, 2 * columns) if turned else (2, 2 * rows, columns)
    near = pl.pallas_call(
        lambda *refs: near_kernel(turned, *refs),
        out_shape=jax.ShapeDtypeStruct(shape, block.dtype),
        in_specs=[SCALARS] + [ANY] * 4,
        out_specs=ANY,
        scratch_shapes=[pltpu.SemaphoreType.DMA((4,))],
        compiler_params=PARAMS,
    )(where, *pieces)
    left = shifted(near, X, 1)
    right = shifted(near, X, -1)
    far = folded(jnp.where(where[C] == 0, right, left))
    own = [near, left, right, far]
    return own + [shifted(piece, C, 1) for piece in own]


def fetch(where, pieces, panel, sems):
    copies = []
    for i, step in enumerate(STEPS):
        for j in range(2):
            copies.append(
                pltpu.make_async_copy(
                    pieces[i + 4 * j],
                    panel.at[where[C] ^ j, x_slot(where, step)],
                    sems.at[i, j],
                )
            )
            copies[-1].start()
    return copies


def dot(a, b):
    return jnp.dot(a, b, preferred_element_type=jnp.float32)


def rotate_kernel(where, *refs):
    pieces, (basis_act, basis_grad), outs = refs[:8], refs[8:10], refs[10:14]
    panel, act, grad, parts, in_sems, basis_sems, out_sems = refs[14:]
    n = act.shape[1]
    first = pltpu.make_async_copy(basis_act, act, basis_sems.at[0])
    second = pltpu.make_async_copy(basis_grad, grad, basis_sems.at[1])
    first.start()
    second.start()
    copies = fetch(where, pieces, panel, in_sems)
    first.wait()
    second.wait()
    for i, step in enumerate(STEPS):
        copies[2 * i].wait()
        copies[2 * i + 1].wait()
        slot = x_slot(where, step)
        for basis, low, k in ((act, 0, n), (grad, n, 2 * n)):
            total = None
            for h in range(2):
                for c in range(2):
                    rows = basis[(2 * h + c) * k:(2 * h + c + 1) * k, :]
                    term = dot(panel[c, slot, h, :, low:low + k], rows)
                    total = term if total is None else total + term
            parts[i, :, low:low + k] = total
        for j, y_step in enumerate(STEPS):
            @pl.when(slot == ((where[Y] + y_step) & 3))
            def _():
                pltpu.make_async_copy(parts.at[i], outs[j], out_sems.at[i]).start()
    for i in range(4):
        pltpu.make_async_copy(parts.at[i], outs[0], out_sems.at[i]).wait()


def rotate(where, pieces, basis_act, basis_grad):
    rows, k = pieces[0].shape[1:]
    f32, bf16 = jnp.float32, jnp.bfloat16
    return pl.pallas_call(
        rotate_kernel,
        out_shape=[jax.ShapeDtypeStruct((rows, k), f32)] * 4,
        in_specs=[SCALARS] + [ANY] * 10,
        out_specs=[ANY] * 4,
        scratch_shapes=[
            pltpu.VMEM((2, 4, 2, rows, k), bf16),
            pltpu.VMEM(basis_act.shape, bf16),
            pltpu.VMEM(basis_grad.shape, bf16),
            pltpu.VMEM((4, rows, k), f32),
            pltpu.SemaphoreType.DMA((4, 2)),
            pltpu.SemaphoreType.DMA((2,)),
            pltpu.SemaphoreType.DMA((4,)),
        ],
        compiler_params=PARAMS,
        cost_estimate=pl.CostEstimate(flops=3 * 10**9, bytes_accessed=12 * 10**6, transcendentals=0),
    )(where, *pieces, basis_act, basis_grad)


def covariance_kernel(where, *refs):
    pieces, mine, outs = refs[:8], refs[8:12], refs[12:14]
    panel, own, act, grad, in_sems, own_sems, out_sems = refs[14:]
    n = act.shape[1]
    tokens = mine[0].shape[1]
    copies = []
    for i, step in enumerate(STEPS):
        span = pl.ds(pl.multiple_of(y_slot(where, step) * tokens, tokens), tokens)
        copies.append(pltpu.make_async_copy(mine[i], own.at[:, span], own_sems.at[i]))
        copies[-1].start()
    copies += fetch(where, pieces, panel, in_sems)
    for copy in copies:
        copy.wait()
    scale = 1.0 / (4 * tokens)
    waits = []
    for h in range(2):
        for c in range(2):
            block = 2 * h + c
            for j, (held, out, low, k) in enumerate(((act, outs[0], 0, n), (grad, outs[1], n, 2 * n))):
                total = None
                for y in range(4):
                    term = dot(
                        own[low:low + k, y * tokens:(y + 1) * tokens],
                        panel[c, y, h, :, low:low + k],
                    )
                    total = term if total is None else total + term
                held[block] = total * scale
                waits.append(
                    pltpu.make_async_copy(
                        held.at[block], out.at[:, block * k:(block + 1) * k], out_sems.at[block, j]
                    )
                )
                waits[-1].start()
    for copy in waits:
        copy.wait()


def covariance(where, pieces, mine):
    rows, k = pieces[0].shape[1:]
    n = k // 3
    f32, bf16 = jnp.float32, jnp.bfloat16
    return pl.pallas_call(
        covariance_kernel,
        out_shape=[
            jax.ShapeDtypeStruct((n, 4 * n), f32),
            jax.ShapeDtypeStruct((2 * n, 8 * n), f32),
        ],
        in_specs=[SCALARS] + [ANY] * 12,
        out_specs=[ANY] * 2,
        scratch_shapes=[
            pltpu.VMEM((2, 4, 2, rows, k), bf16),
            pltpu.VMEM((k, 4 * rows), bf16),
            pltpu.VMEM((4, n, n), f32),
            pltpu.VMEM((4, 2 * n, 2 * n), f32),
            pltpu.SemaphoreType.DMA((4, 2)),
            pltpu.SemaphoreType.DMA((4,)),
            pltpu.SemaphoreType.DMA((4, 2)),
        ],
        compiler_params=PARAMS,
        cost_estimate=pl.CostEstimate(flops=3 * 10**9, bytes_accessed=14 * 10**6, transcendentals=0),
    )(where, *pieces, *mine)


def correction_kernel(where, *refs):
    pieces, squares, out = refs[:8], refs[8:12], refs[12]
    panel, grad, held, in_sems, grad_sems, out_sems = refs[13:]
    rows, tokens = panel.shape[3:]
    copies = fetch(where, pieces, panel, in_sems)
    for i, step in enumerate(STEPS):
        copies.append(
            pltpu.make_async_copy(squares[i], grad.at[y_slot(where, step)], grad_sems.at[i])
        )
        copies[-1].start()
    for copy in copies:
        copy.wait()
    scale = 1.0 / (4 * tokens)
    waits = []
    for h in range(2):
        for c in range(2):
            block = 2 * h + c
            total = None
            for y in range(4):
                term = dot(panel[c, y, h], grad[y])
                total = term if total is None else total + term
            held[block] = total * scale
            waits.append(
                pltpu.make_async_copy(
                    held.at[block], out.at[block * rows:(block + 1) * rows, :], out_sems.at[block]
                )
            )
            waits[-1].start()
    for copy in waits:
        copy.wait()


def correct(where, pieces, squares):
    rows, tokens = pieces[0].shape[1:]
    n = squares[0].shape[1]
    f32, bf16 = jnp.float32, jnp.bfloat16
    return pl.pallas_call(
        correction_kernel,
        out_shape=jax.ShapeDtypeStruct((4 * rows, n), f32),
        in_specs=[SCALARS] + [ANY] * 12,
        out_specs=ANY,
        scratch_shapes=[
            pltpu.VMEM((2, 4, 2, rows, tokens), bf16),
            pltpu.VMEM((4, tokens, n), bf16),
            pltpu.VMEM((4, rows, n), f32),
            pltpu.SemaphoreType.DMA((4, 2)),
            pltpu.SemaphoreType.DMA((4,)),
            pltpu.SemaphoreType.DMA((4,)),
        ],
        compiler_params=PARAMS,
        cost_estimate=pl.CostEstimate(flops=10**9, bytes_accessed=5 * 10**6, transcendentals=0),
    )(where, *pieces, *squares)


def square_kernel(part_ref, arrived_ref, act_ref, grad_ref):
    n = act_ref.shape[0]
    total = part_ref[...] + arrived_ref[...]
    square = total * total
    act_ref[...] = square[:, :n].T.astype(jnp.bfloat16)
    grad_ref[...] = square[:, n:].astype(jnp.bfloat16)


def pair_up(block, where, axis):
    other = shifted(block, ZL, 1)
    low = where[ZL] == 0
    return jnp.concatenate([jnp.where(low, block, other), jnp.where(low, other, block)], axis=axis)


def body(tokens, out_grads, basis_act, basis_grad):
    where = jnp.stack([lax.axis_index(axis) for axis in AXES]).astype(jnp.int32)
    n = tokens.shape[1]
    mine = jnp.concatenate([tokens, out_grads], axis=1)
    panel = gather_group(mine, where, False)
    turned = pair_up(mine.T, where, 1)
    own = [turned if step == 0 else shifted(turned, Y, step) for step in STEPS]
    parts = rotate(where, panel, basis_act, basis_grad)
    cov_act, cov_grad = covariance(where, panel, own)
    parts = [part.reshape(2, -1, 3 * n) for part in parts]
    parts = [part if step == 0 else shifted(part, Y, step) for step, part in zip(STEPS, parts)]

    def half(which):
        return sum(lax.dynamic_index_in_dim(part, which, 0, False) for part in parts)

    arrived = shifted(half(1 - where[ZL]), ZL, 1)
    kept = half(where[ZL])
    sq_act, sq_grad = pl.pallas_call(
        square_kernel,
        out_shape=[
            jax.ShapeDtypeStruct((n, kept.shape[0]), jnp.bfloat16),
            jax.ShapeDtypeStruct((kept.shape[0], 2 * n), jnp.bfloat16),
        ],
    )(kept, arrived)
    squares = gather_group(sq_act, where, True)
    pair = pair_up(sq_grad, where, 0)
    square_own = [pair if step == 0 else shifted(pair, Y, step) for step in STEPS]
    correction = correct(where, squares, square_own)
    return (cov_act, cov_grad, correction)


def solution(mesh):
    fine = Mesh(mesh.devices.reshape(SIZES), AXES)
    dp, tensor = ("zl", "y"), ("x", "zh", "c")
    placed = P(dp, tensor)
    return jax.shard_map(
        body,
        mesh=fine,
        in_specs=(placed,) * 4,
        out_specs=(P(tensor, dp), P(tensor, dp), placed),
        check_vma=False,
    )
```

```python
import itertools

import jax
import jax.numpy as jnp
from jax import lax
from jax.experimental import pallas as pl
from jax.experimental.pallas import tpu as pltpu
from jax.sharding import Mesh, PartitionSpec as P

AXES = ("zl", "y", "x", "zh", "c")
SIZES = (2, 4, 4, 4, 2)
ZL, Y, X, ZH, C = range(5)
STEPS = (0, 1, -1, 2)
ANY = pl.BlockSpec(memory_space=pl.ANY)
WHOLE = pl.BlockSpec(memory_space=pltpu.VMEM)
SCALARS = pl.BlockSpec(memory_space=pltpu.SMEM)
PARAMS = pltpu.CompilerParams(vmem_limit_bytes=48 * 1024 * 1024)

CHEAP = pl.CostEstimate(flops=1000, bytes_accessed=1000, transcendentals=0)


def device_index(q):
    index = 0
    for size, value in zip(SIZES, q):
        index = index * size + value
    return index


def permutation(target):
    every = itertools.product(*(range(size) for size in SIZES))
    return [(device_index(q), device_index(target(*q))) for q in every]


def shifted(value, axis, step):
    def target(*q):
        q = list(q)
        q[axis] = (q[axis] + step) % SIZES[axis]
        return q

    return lax.ppermute(value, AXES, permutation(target))


def direct(value, axis):
    return [value if step == 0 else shifted(value, axis, step) for step in STEPS]


def to_group(zl, y, x, zh, c):
    row = (x & 1) * 2 + (zh >> 1)
    flip = zl ^ (x >> 1)
    return x >> 1, row, x ^ y ^ row, ((zh >> 1) ^ flip) * 2 + ((zh & 1) ^ flip), c


def x_slot(where, step):
    return ((where[X] - step) & 3) ^ (where[ZL] * 2 + (where[Y] >> 1)) ^ where[Y]


def y_slot(where, step):
    return (where[Y] - step) & 3


def z_slot(where, step):
    slot = (where[ZH] - step) & 3
    flip = (slot >> 1) ^ (where[Y] & 1)
    return flip ^ where[ZL], (slot & 1) ^ flip


def near_kernel(turned, where, *refs):
    pieces, near, sems = refs[:4], refs[-2], refs[-1]
    copies = []
    for i, (step, piece) in enumerate(zip(STEPS, pieces)):
        zl, h = z_slot(where, step)
        tokens = piece.shape[1 if turned else 0]
        span = pl.ds(pl.multiple_of(zl * tokens, tokens), tokens)
        target = near.at[h, :, span] if turned else near.at[h, span, :]
        copies.append(pltpu.make_async_copy(piece, target, sems.at[i]))
        copies[-1].start()
    for copy in copies:
        copy.wait()


def gather_near(block, where, turned, after):
    rows, columns = block.shape
    shape = (2, rows, 2 * columns) if turned else (2, 2 * rows, columns)
    return pl.pallas_call(
        lambda *refs: near_kernel(turned, *refs),
        out_shape=jax.ShapeDtypeStruct(shape, block.dtype),
        in_specs=[SCALARS] + [ANY] * (4 + len(after)),
        out_specs=ANY,
        scratch_shapes=[pltpu.SemaphoreType.DMA((4,))],
        compiler_params=PARAMS,
        cost_estimate=CHEAP,
    )(where, *direct(block, ZH), *after)


def stack_kernel(where, *refs):
    *pieces, stack, sems = refs
    copies = []
    for i, (step, piece) in enumerate(zip(STEPS, pieces)):
        copies.append(pltpu.make_async_copy(piece, stack.at[y_slot(where, step)], sems.at[i]))
        copies[-1].start()
    for copy in copies:
        copy.wait()


def stack_up(where, pieces):
    return pl.pallas_call(
        stack_kernel,
        out_shape=jax.ShapeDtypeStruct((4,) + pieces[0].shape, pieces[0].dtype),
        in_specs=[SCALARS] + [ANY] * 4,
        out_specs=ANY,
        scratch_shapes=[pltpu.SemaphoreType.DMA((4,))],
        compiler_params=PARAMS,
        cost_estimate=CHEAP,
    )(where, *pieces)


def gather_far(near):
    own = direct(near, X)
    return own + [shifted(piece, C, 1) for piece in own]


def fetch(where, pieces, panel, sems):
    copies = []
    for i, step in enumerate(STEPS):
        for j in range(2):
            copies.append(
                pltpu.make_async_copy(
                    pieces[i + 4 * j],
                    panel.at[where[C] ^ j, x_slot(where, step)],
                    sems.at[i, j],
                )
            )
            copies[-1].start()
    return copies


def dot(a, b):
    return jnp.dot(a, b, preferred_element_type=jnp.float32)


def encode(value, out, low):
    rows, n = value.shape
    top = jnp.max(jnp.max(jnp.abs(value), axis=0, keepdims=True), axis=1, keepdims=True)
    top = jnp.maximum(top, 1e-30).astype(jnp.bfloat16)
    power = value * (32768.0 / top.astype(jnp.float32))
    sign = power < 0
    for _ in range(3):
        power = power * power
    out[:rows, low:low + n] = jnp.where(sign, -power, power).astype(jnp.bfloat16)
    out[rows:, low:low + n] = jnp.broadcast_to(top, (16, n))


def decode(coded):
    rows = coded.shape[0] - 16
    power = coded[:rows, :].astype(jnp.float32)
    top = coded[rows:rows + 1, :].astype(jnp.float32) * (1.0 / 32768.0)
    root = jnp.abs(power)
    for _ in range(3):
        root = jnp.sqrt(root)
    return jnp.where(power < 0, -root, root) * top


def rotate_kernel(where, *refs):
    pieces, (act_ref, grad_ref), outs = refs[:8], refs[8:10], refs[-9:-5]
    panel, act, grad, in_sems, basis_sems = refs[-5:]
    n = act.shape[1]
    loads = [
        pltpu.make_async_copy(act_ref, act, basis_sems.at[0]),
        pltpu.make_async_copy(grad_ref, grad, basis_sems.at[1]),
    ]
    for load in loads:
        load.start()
    for copy in loads + fetch(where, pieces, panel, in_sems):
        copy.wait()
    for out, step in zip(outs, STEPS):
        slot = (where[Y] + step) & 3
        for basis, low, k in ((act, 0, n), (grad, n, 2 * n)):
            total = None
            for h in range(2):
                for c in range(2):
                    rows = basis[(2 * h + c) * k:(2 * h + c + 1) * k, :]
                    term = dot(panel[c, slot, h, :, low:low + k], rows)
                    total = term if total is None else total + term
            if step == 0:
                out[:, low:low + k] = total
            else:
                encode(total, out, low)


def rotate(where, pieces, basis_act, basis_grad, after):
    rows, k = pieces[0].shape[1:]
    f32, bf16 = jnp.float32, jnp.bfloat16
    return pl.pallas_call(
        rotate_kernel,
        out_shape=[jax.ShapeDtypeStruct((rows, k), f32)]
        + [jax.ShapeDtypeStruct((rows + 16, k), bf16)] * 3,
        in_specs=[SCALARS] + [ANY] * (10 + len(after)),
        scratch_shapes=[
            pltpu.VMEM((2, 4, 2, rows, k), bf16),
            pltpu.VMEM(basis_act.shape, bf16),
            pltpu.VMEM(basis_grad.shape, bf16),
            pltpu.SemaphoreType.DMA((4, 2)),
            pltpu.SemaphoreType.DMA((2,)),
        ],
        compiler_params=PARAMS,
        cost_estimate=CHEAP,
    )(where, *pieces, basis_act, basis_grad, *after)


def covariance_kernel(where, *refs):
    pieces, stacks, outs, token = refs[:8], refs[8:10], refs[10:12], refs[12]
    panel, own, act, grad, in_sems, own_sems, out_sems = refs[13:]
    token[...] = jnp.zeros_like(token)
    n = act.shape[1]
    rows = stacks[0].shape[2]
    tokens = 2 * rows
    copies = []
    for i, stack in enumerate(stacks):
        for y in range(4):
            start = pl.multiple_of((2 * y + (where[ZL] ^ i)) * rows, rows)
            copies.append(
                pltpu.make_async_copy(stack.at[y], own.at[:, pl.ds(start, rows)], own_sems.at[i, y])
            )
            copies[-1].start()
    copies += fetch(where, pieces, panel, in_sems)
    for copy in copies:
        copy.wait()
    scale = 1.0 / (4 * tokens)
    waits = []
    for h in range(2):
        for c in range(2):
            block = 2 * h + c
            for j, (held, out, low, k) in enumerate(((act, outs[0], 0, n), (grad, outs[1], n, 2 * n))):
                total = None
                for y in range(4):
                    term = dot(
                        own[low:low + k, y * tokens:(y + 1) * tokens],
                        panel[c, y, h, :, low:low + k],
                    )
                    total = term if total is None else total + term
                held[block] = total * scale
                waits.append(
                    pltpu.make_async_copy(
                        held.at[block], out.at[:, block * k:(block + 1) * k], out_sems.at[block, j]
                    )
                )
                waits[-1].start()
    for copy in waits:
        copy.wait()


def covariance(where, pieces, mine):
    rows, k = pieces[0].shape[1:]
    n = k // 3
    f32, bf16 = jnp.float32, jnp.bfloat16
    return pl.pallas_call(
        covariance_kernel,
        out_shape=[
            jax.ShapeDtypeStruct((n, 4 * n), f32),
            jax.ShapeDtypeStruct((2 * n, 8 * n), f32),
            jax.ShapeDtypeStruct((8, 128), f32),
        ],
        in_specs=[SCALARS] + [ANY] * 10,
        out_specs=[ANY] * 2 + [WHOLE],
        scratch_shapes=[
            pltpu.VMEM((2, 4, 2, rows, k), bf16),
            pltpu.VMEM((k, 4 * rows), bf16),
            pltpu.VMEM((4, n, n), f32),
            pltpu.VMEM((4, 2 * n, 2 * n), f32),
            pltpu.SemaphoreType.DMA((4, 2)),
            pltpu.SemaphoreType.DMA((2, 4)),
            pltpu.SemaphoreType.DMA((4, 2)),
        ],
        compiler_params=PARAMS,
        cost_estimate=CHEAP,
    )(where, *pieces, *mine)


def correction_kernel(where, *refs):
    pieces, squares, out = refs[:8], refs[8:12], refs[12]
    panel, grad, held, in_sems, grad_sems, out_sems = refs[13:]
    rows, tokens = panel.shape[3:]
    copies = fetch(where, pieces, panel, in_sems)
    for i, step in enumerate(STEPS):
        copies.append(
            pltpu.make_async_copy(squares[i], grad.at[y_slot(where, step)], grad_sems.at[i])
        )
        copies[-1].start()
    for copy in copies:
        copy.wait()
    scale = 1.0 / (4 * tokens)
    waits = []
    for h in range(2):
        for c in range(2):
            block = 2 * h + c
            total = None
            for y in range(4):
                term = dot(panel[c, y, h], grad[y])
                total = term if total is None else total + term
            held[block] = total * scale
            waits.append(
                pltpu.make_async_copy(
                    held.at[block], out.at[block * rows:(block + 1) * rows, :], out_sems.at[block]
                )
            )
            waits[-1].start()
    for copy in waits:
        copy.wait()


def correct(where, pieces, squares):
    rows, tokens = pieces[0].shape[1:]
    n = squares[0].shape[1]
    f32, bf16 = jnp.float32, jnp.bfloat16
    return pl.pallas_call(
        correction_kernel,
        out_shape=jax.ShapeDtypeStruct((4 * rows, n), f32),
        in_specs=[SCALARS] + [ANY] * 12,
        out_specs=ANY,
        scratch_shapes=[
            pltpu.VMEM((2, 4, 2, rows, tokens), bf16),
            pltpu.VMEM((4, tokens, n), bf16),
            pltpu.VMEM((4, rows, n), f32),
            pltpu.SemaphoreType.DMA((4, 2)),
            pltpu.SemaphoreType.DMA((4,)),
            pltpu.SemaphoreType.DMA((4,)),
        ],
        compiler_params=PARAMS,
        cost_estimate=CHEAP,
    )(where, *pieces, *squares)


def half_kernel(where, own, *refs):
    arrived, kept, sent, total = refs[:3], refs[-3], refs[-2], refs[-1]
    rows = kept.shape[0]
    whole = own[...]
    for coded in arrived:
        whole = whole + decode(coded)
    for i in range(2):
        total[i] = whole[i * rows:(i + 1) * rows]
    kept[...] = total[where[ZL]]
    n = kept.shape[1] // 3
    other = total[1 - where[ZL]]
    encode(other[:, :n], sent, 0)
    encode(other[:, n:], sent, n)


def sum_over_y(parts, where, after=()):
    rows, n = parts[0].shape
    rows = rows // 2
    parts = [part if step == 0 else shifted(part, Y, step) for step, part in zip(STEPS, parts)]
    return pl.pallas_call(
        half_kernel,
        out_shape=[
            jax.ShapeDtypeStruct((rows, n), jnp.float32),
            jax.ShapeDtypeStruct((rows + 16, n), jnp.bfloat16),
        ],
        in_specs=[SCALARS] + [WHOLE] * 4 + [ANY] * len(after),
        scratch_shapes=[pltpu.VMEM((2, rows, n), jnp.float32)],
        compiler_params=PARAMS,
        cost_estimate=CHEAP,
    )(where, *parts, *after)


def square_kernel(kept, arrived, act, grad):
    n = act.shape[0]
    total = kept[...] + decode(arrived)
    square = total * total
    act[...] = square[:, :n].T.astype(jnp.bfloat16)
    grad[...] = square[:, n:].astype(jnp.bfloat16)


def square_of_sum(kept, sent):
    rows, n = kept.shape[0], kept.shape[1] // 3
    return pl.pallas_call(
        square_kernel,
        out_shape=[
            jax.ShapeDtypeStruct((n, rows), jnp.bfloat16),
            jax.ShapeDtypeStruct((rows, 2 * n), jnp.bfloat16),
        ],
        compiler_params=PARAMS,
        cost_estimate=CHEAP,
    )(kept, shifted(sent, ZL, 1))


def pair_kernel(axis, where, own, other, pair, sems):
    size = own.shape[axis]
    copies = []
    for i, (ref, zl) in enumerate(((own, where[ZL]), (other, 1 - where[ZL]))):
        span = pl.ds(pl.multiple_of(zl * size, size), size)
        target = pair.at[:, span] if axis else pair.at[span, :]
        copies.append(pltpu.make_async_copy(ref, target, sems.at[i]))
        copies[-1].start()
    for copy in copies:
        copy.wait()


def pair_up(block, where, axis):
    shape = list(block.shape)
    shape[axis] *= 2
    return pl.pallas_call(
        lambda *refs: pair_kernel(axis, *refs),
        out_shape=jax.ShapeDtypeStruct(shape, block.dtype),
        in_specs=[SCALARS] + [ANY] * 2,
        out_specs=ANY,
        scratch_shapes=[pltpu.SemaphoreType.DMA((2,))],
        compiler_params=PARAMS,
        cost_estimate=CHEAP,
    )(where, block, shifted(block, ZL, 1))


def prepare_kernel(tokens, out_grads, joined, turned):
    n = tokens.shape[1]
    joined[:, :n] = tokens[...]
    joined[:, n:] = out_grads[...]
    turned[:n, :] = tokens[...].T
    turned[n:, :] = out_grads[...].T


def prepare(tokens, out_grads):
    rows, k = tokens.shape[0], tokens.shape[1] + out_grads.shape[1]
    return pl.pallas_call(
        prepare_kernel,
        out_shape=[
            jax.ShapeDtypeStruct((rows, k), tokens.dtype),
            jax.ShapeDtypeStruct((k, rows), tokens.dtype),
        ],
        compiler_params=PARAMS,
        cost_estimate=CHEAP,
    )(tokens, out_grads)


def in_order(first, *later):
    return lax.optimization_barrier((first, *later))[1:]


def body(tokens, out_grads, basis_act, basis_grad):
    where = jnp.stack([lax.axis_index(axis) for axis in AXES]).astype(jnp.int32)
    joined, turned = prepare(tokens, out_grads)
    block = lax.ppermute(joined, AXES, permutation(to_group))
    (turned,) = in_order(block, turned)
    own = direct(turned, Y)
    near = gather_near(block, where, False, own[1:])
    stack = stack_up(where, own)
    panel = gather_far(near)
    stacks = (stack, shifted(stack, ZL, 1))
    parts = rotate(where, panel, basis_act, basis_grad, stacks)
    cov_act, cov_grad, done = covariance(where, panel, stacks)
    sq_act, sq_grad = square_of_sum(*sum_over_y(parts, where, (done,)))
    block = lax.ppermute(sq_act, AXES, permutation(to_group))
    pair = pair_up(sq_grad, where, 0)
    pair, block = lax.optimization_barrier((pair, block))
    squares_own = direct(pair, Y)
    squares = gather_far(gather_near(block, where, True, squares_own[1:3]))
    correction = correct(where, squares, squares_own)
    return (cov_act, cov_grad, correction)


def solution(mesh):
    fine = Mesh(mesh.devices.reshape(SIZES), AXES)
    dp, tensor = ("zl", "y"), ("x", "zh", "c")
    placed = P(dp, tensor)
    return jax.shard_map(
        body,
        mesh=fine,
        in_specs=(placed,) * 4,
        out_specs=(P(tensor, dp), P(tensor, dp), placed),
        check_vma=False,
    )
```

```python
import itertools

import jax
import jax.numpy as jnp
from jax import lax
from jax.experimental import pallas as pl
from jax.experimental.pallas import tpu as pltpu
from jax.sharding import Mesh, PartitionSpec as P

AXES = ("zl", "y", "x", "zh", "c")
SIZES = (2, 4, 4, 4, 2)
ZL, Y, X, ZH, C = range(5)
STEPS = (0, 1, -1, 2)
ANY = pl.BlockSpec(memory_space=pl.ANY)
WHOLE = pl.BlockSpec(memory_space=pltpu.VMEM)
SCALARS = pl.BlockSpec(memory_space=pltpu.SMEM)
PARAMS = pltpu.CompilerParams(vmem_limit_bytes=48 * 1024 * 1024)

CHEAP = pl.CostEstimate(flops=1000, bytes_accessed=1000, transcendentals=0)


def device_index(q):
    index = 0
    for size, value in zip(SIZES, q):
        index = index * size + value
    return index


def permutation(target):
    every = itertools.product(*(range(size) for size in SIZES))
    return [(device_index(q), device_index(target(*q))) for q in every]


def shifted(value, axis, step):
    def target(*q):
        q = list(q)
        q[axis] = (q[axis] + step) % SIZES[axis]
        return q

    return lax.ppermute(value, AXES, permutation(target))


def direct(value, axis):
    return [value if step == 0 else shifted(value, axis, step) for step in STEPS]


def folded(value):
    def target(zl, y, x, zh, c):
        return zl, y, (x - 1 + 2 * c) % SIZES[X], zh, c

    return lax.ppermute(value, AXES, permutation(target))


def to_group(zl, y, x, zh, c):
    row = (x & 1) * 2 + (zh >> 1)
    flip = zl ^ (x >> 1)
    return x >> 1, row, x ^ y ^ row, ((zh >> 1) ^ flip) * 2 + ((zh & 1) ^ flip), c


def x_slot(where, step):
    return ((where[X] - step) & 3) ^ (where[ZL] * 2 + (where[Y] >> 1)) ^ where[Y]


def y_slot(where, step):
    return (where[Y] - step) & 3


def z_slot(where, step):
    slot = (where[ZH] - step) & 3
    flip = (slot >> 1) ^ (where[Y] & 1)
    return flip ^ where[ZL], (slot & 1) ^ flip


def near_kernel(turned, where, *refs):
    pieces, near, sems = refs[:4], refs[-2], refs[-1]
    copies = []
    for i, (step, piece) in enumerate(zip(STEPS, pieces)):
        zl, h = z_slot(where, step)
        tokens = piece.shape[1 if turned else 0]
        span = pl.ds(pl.multiple_of(zl * tokens, tokens), tokens)
        target = near.at[h, :, span] if turned else near.at[h, span, :]
        copies.append(pltpu.make_async_copy(piece, target, sems.at[i]))
        copies[-1].start()
    for copy in copies:
        copy.wait()


def gather_near(block, where, turned, after):
    rows, columns = block.shape
    shape = (2, rows, 2 * columns) if turned else (2, 2 * rows, columns)
    return pl.pallas_call(
        lambda *refs: near_kernel(turned, *refs),
        out_shape=jax.ShapeDtypeStruct(shape, block.dtype),
        in_specs=[SCALARS] + [ANY] * (4 + len(after)),
        out_specs=ANY,
        scratch_shapes=[pltpu.SemaphoreType.DMA((4,))],
        compiler_params=PARAMS,
        cost_estimate=CHEAP,
    )(where, *direct(block, ZH), *after)


def stack_kernel(where, *refs):
    *pieces, stack, sems = refs
    copies = []
    for i, (step, piece) in enumerate(zip(STEPS, pieces)):
        copies.append(pltpu.make_async_copy(piece, stack.at[y_slot(where, step)], sems.at[i]))
        copies[-1].start()
    for copy in copies:
        copy.wait()


def stack_up(where, pieces):
    return pl.pallas_call(
        stack_kernel,
        out_shape=jax.ShapeDtypeStruct((4,) + pieces[0].shape, pieces[0].dtype),
        in_specs=[SCALARS] + [ANY] * 4,
        out_specs=ANY,
        scratch_shapes=[pltpu.SemaphoreType.DMA((4,))],
        compiler_params=PARAMS,
        cost_estimate=CHEAP,
    )(where, *pieces)


def gather_far(near, where=None, after=None):
    if where is None:
        own = direct(near, X)
    else:
        left, right = shifted(near, X, 1), shifted(near, X, -1)
        _, passed = lax.optimization_barrier((after, jnp.where(where[C] == 0, right, left)))
        own = [near, left, right, folded(passed)]
    return own + [shifted(piece, C, 1) for piece in own]


def fetch(where, pieces, panel, sems):
    copies = []
    for i, step in enumerate(STEPS):
        for j in range(2):
            copies.append(
                pltpu.make_async_copy(
                    pieces[i + 4 * j],
                    panel.at[where[C] ^ j, x_slot(where, step)],
                    sems.at[i, j],
                )
            )
            copies[-1].start()
    return copies


def dot(a, b):
    return jnp.dot(a, b, preferred_element_type=jnp.float32)


def encode(value, out):
    rows, n = value.shape
    top = jnp.max(jnp.max(jnp.abs(value), axis=0, keepdims=True), axis=1, keepdims=True)
    top = jnp.maximum(top, 1e-30).astype(jnp.bfloat16)
    power = value * (32768.0 / top.astype(jnp.float32))
    sign = power < 0
    for _ in range(3):
        power = power * power
    out[:rows, :] = jnp.where(sign, -power, power).astype(jnp.bfloat16)
    out[rows:, :] = jnp.broadcast_to(top, (16, n))


def decode(coded):
    rows = coded.shape[0] - 16
    power = coded[:rows, :].astype(jnp.float32)
    top = coded[rows:rows + 1, :].astype(jnp.float32) * (1.0 / 32768.0)
    root = jnp.abs(power)
    for _ in range(3):
        root = jnp.sqrt(root)
    return jnp.where(power < 0, -root, root) * top


def rotate_kernel(where, *refs):
    pieces, (act_ref, grad_ref) = refs[:8], refs[8:10]
    outs, act_kept, act_sent = refs[-12:-8], refs[-8], refs[-7]
    panel, act, grad, held, in_sems, basis_sems = refs[-6:]
    n = act.shape[1]
    loads = [
        pltpu.make_async_copy(act_ref, act, basis_sems.at[0]),
        pltpu.make_async_copy(grad_ref, grad, basis_sems.at[1]),
    ]
    for load in loads:
        load.start()
    for copy in loads + fetch(where, pieces, panel, in_sems):
        copy.wait()

    def product(basis, low, k, slot):
        total = None
        for h in range(2):
            for c in range(2):
                rows = basis[(2 * h + c) * k:(2 * h + c + 1) * k, :]
                term = dot(panel[c, slot, h, :, low:low + k], rows)
                total = term if total is None else total + term
        return total

    rows = act_kept.shape[1]
    for i, (out, step) in enumerate(zip(outs, STEPS)):
        slot = (where[Y] + step) & 3
        total = product(grad, n, 2 * n, slot)
        if step == 0:
            out[...] = total
        else:
            encode(total, out)
        total = product(act, 0, n, slot)
        held[0, i] = total[:rows]
        held[1, i] = total[rows:]
    act_kept[...] = held[where[ZL]]
    encode(held[1 - where[ZL]].reshape(4 * rows, n), act_sent)


def rotate(where, pieces, basis_act, basis_grad, after):
    rows, k = pieces[0].shape[1:]
    n = k // 3
    f32, bf16 = jnp.float32, jnp.bfloat16
    return pl.pallas_call(
        rotate_kernel,
        out_shape=[jax.ShapeDtypeStruct((rows, 2 * n), f32)]
        + [jax.ShapeDtypeStruct((rows + 16, 2 * n), bf16)] * 3
        + [
            jax.ShapeDtypeStruct((4, rows // 2, n), f32),
            jax.ShapeDtypeStruct((2 * rows + 16, n), bf16),
        ],
        in_specs=[SCALARS] + [ANY] * (10 + len(after)),
        scratch_shapes=[
            pltpu.VMEM((2, 4, 2, rows, k), bf16),
            pltpu.VMEM(basis_act.shape, bf16),
            pltpu.VMEM(basis_grad.shape, bf16),
            pltpu.VMEM((2, 4, rows // 2, n), f32),
            pltpu.SemaphoreType.DMA((4, 2)),
            pltpu.SemaphoreType.DMA((2,)),
        ],
        compiler_params=PARAMS,
        cost_estimate=CHEAP,
    )(where, *pieces, basis_act, basis_grad, *after)


def covariance_kernel(where, *refs):
    pieces, stacks, outs, token = refs[:8], refs[8:10], refs[10:12], refs[12]
    panel, own, act, grad, in_sems, own_sems, out_sems = refs[13:]
    token[...] = jnp.zeros_like(token)
    n = act.shape[1]
    rows = stacks[0].shape[2]
    tokens = 2 * rows
    copies = []
    for i, stack in enumerate(stacks):
        for y in range(4):
            start = pl.multiple_of((2 * y + (where[ZL] ^ i)) * rows, rows)
            copies.append(
                pltpu.make_async_copy(stack.at[y], own.at[:, pl.ds(start, rows)], own_sems.at[i, y])
            )
            copies[-1].start()
    copies += fetch(where, pieces, panel, in_sems)
    for copy in copies:
        copy.wait()
    scale = 1.0 / (4 * tokens)
    waits = []
    for h in range(2):
        for c in range(2):
            block = 2 * h + c
            for j, (held, out, low, k) in enumerate(((act, outs[0], 0, n), (grad, outs[1], n, 2 * n))):
                total = None
                for y in range(4):
                    term = dot(
                        own[low:low + k, y * tokens:(y + 1) * tokens],
                        panel[c, y, h, :, low:low + k],
                    )
                    total = term if total is None else total + term
                held[block] = total * scale
                waits.append(
                    pltpu.make_async_copy(
                        held.at[block], out.at[:, block * k:(block + 1) * k], out_sems.at[block, j]
                    )
                )
                waits[-1].start()
    for copy in waits:
        copy.wait()


def covariance(where, pieces, mine):
    rows, k = pieces[0].shape[1:]
    n = k // 3
    f32, bf16 = jnp.float32, jnp.bfloat16
    return pl.pallas_call(
        covariance_kernel,
        out_shape=[
            jax.ShapeDtypeStruct((n, 4 * n), f32),
            jax.ShapeDtypeStruct((2 * n, 8 * n), f32),
            jax.ShapeDtypeStruct((8, 128), f32),
        ],
        in_specs=[SCALARS] + [ANY] * 10,
        out_specs=[ANY] * 2 + [WHOLE],
        scratch_shapes=[
            pltpu.VMEM((2, 4, 2, rows, k), bf16),
            pltpu.VMEM((k, 4 * rows), bf16),
            pltpu.VMEM((4, n, n), f32),
            pltpu.VMEM((4, 2 * n, 2 * n), f32),
            pltpu.SemaphoreType.DMA((4, 2)),
            pltpu.SemaphoreType.DMA((2, 4)),
            pltpu.SemaphoreType.DMA((4, 2)),
        ],
        compiler_params=PARAMS,
        cost_estimate=CHEAP,
    )(where, *pieces, *mine)


def correction_kernel(where, *refs):
    pieces, squares, out = refs[:8], refs[8:12], refs[12]
    panel, grad, held, in_sems, grad_sems, out_sems = refs[13:]
    rows, tokens = panel.shape[3:]
    copies = fetch(where, pieces, panel, in_sems)
    for i, step in enumerate(STEPS):
        copies.append(
            pltpu.make_async_copy(squares[i], grad.at[y_slot(where, step)], grad_sems.at[i])
        )
        copies[-1].start()
    for copy in copies:
        copy.wait()
    scale = 1.0 / (4 * tokens)
    waits = []
    for h in range(2):
        for c in range(2):
            block = 2 * h + c
            total = None
            for y in range(4):
                term = dot(panel[c, y, h], grad[y])
                total = term if total is None else total + term
            held[block] = total * scale
            waits.append(
                pltpu.make_async_copy(
                    held.at[block], out.at[block * rows:(block + 1) * rows, :], out_sems.at[block]
                )
            )
            waits[-1].start()
    for copy in waits:
        copy.wait()


def correct(where, pieces, squares):
    rows, tokens = pieces[0].shape[1:]
    n = squares[0].shape[1]
    f32, bf16 = jnp.float32, jnp.bfloat16
    return pl.pallas_call(
        correction_kernel,
        out_shape=jax.ShapeDtypeStruct((4 * rows, n), f32),
        in_specs=[SCALARS] + [ANY] * 12,
        out_specs=ANY,
        scratch_shapes=[
            pltpu.VMEM((2, 4, 2, rows, tokens), bf16),
            pltpu.VMEM((4, tokens, n), bf16),
            pltpu.VMEM((4, rows, n), f32),
            pltpu.SemaphoreType.DMA((4, 2)),
            pltpu.SemaphoreType.DMA((4,)),
            pltpu.SemaphoreType.DMA((4,)),
        ],
        compiler_params=PARAMS,
        cost_estimate=CHEAP,
    )(where, *pieces, *squares)


def half_kernel(where, own, *refs):
    arrived, kept, sent, total = refs[:3], refs[-3], refs[-2], refs[-1]
    rows = kept.shape[0]
    whole = own[...]
    for coded in arrived:
        whole = whole + decode(coded)
    for i in range(2):
        total[i] = whole[i * rows:(i + 1) * rows]
    kept[...] = total[where[ZL]]
    encode(total[1 - where[ZL]], sent)


def sum_over_y(parts, where, after=()):
    rows, n = parts[0].shape
    rows = rows // 2
    parts = [part if step == 0 else shifted(part, Y, step) for step, part in zip(STEPS, parts)]
    return pl.pallas_call(
        half_kernel,
        out_shape=[
            jax.ShapeDtypeStruct((rows, n), jnp.float32),
            jax.ShapeDtypeStruct((rows + 16, n), jnp.bfloat16),
        ],
        in_specs=[SCALARS] + [WHOLE] * 4 + [ANY] * len(after),
        scratch_shapes=[pltpu.VMEM((2, rows, n), jnp.float32)],
        compiler_params=PARAMS,
        cost_estimate=CHEAP,
    )(where, *parts, *after)


def grad_square_kernel(kept, arrived, out):
    total = kept[...] + decode(arrived)
    out[...] = (total * total).astype(jnp.bfloat16)


def grad_squares(kept, sent):
    return pl.pallas_call(
        grad_square_kernel,
        out_shape=jax.ShapeDtypeStruct(kept.shape, jnp.bfloat16),
        compiler_params=PARAMS,
        cost_estimate=CHEAP,
    )(kept, shifted(sent, ZL, 1))


def split_kernel(kept, arrived, *outs):
    rows, n = kept.shape[1:]
    total = kept[...] + decode(arrived).reshape(4, rows, n)
    outs[0][...] = total[0]
    for i in range(1, 4):
        encode(total[i], outs[i])


def act_square_kernel(own, *refs):
    total = own[...]
    for coded in refs[:3]:
        total = total + decode(coded)
    refs[3][...] = (total * total).T.astype(jnp.bfloat16)


def act_squares(kept, sent):
    rows, n = kept.shape[1:]
    parts = pl.pallas_call(
        split_kernel,
        out_shape=[jax.ShapeDtypeStruct((rows, n), jnp.float32)]
        + [jax.ShapeDtypeStruct((rows + 16, n), jnp.bfloat16)] * 3,
        compiler_params=PARAMS,
        cost_estimate=CHEAP,
    )(kept, shifted(sent, ZL, 1))
    return parts[0], pl.pallas_call(
        act_square_kernel,
        out_shape=jax.ShapeDtypeStruct((n, rows), jnp.bfloat16),
        compiler_params=PARAMS,
        cost_estimate=CHEAP,
    )(*[part if step == 0 else shifted(part, Y, step) for step, part in zip(STEPS, parts)])


def pair_kernel(axis, where, own, other, pair, sems):
    size = own.shape[axis]
    copies = []
    for i, (ref, zl) in enumerate(((own, where[ZL]), (other, 1 - where[ZL]))):
        span = pl.ds(pl.multiple_of(zl * size, size), size)
        target = pair.at[:, span] if axis else pair.at[span, :]
        copies.append(pltpu.make_async_copy(ref, target, sems.at[i]))
        copies[-1].start()
    for copy in copies:
        copy.wait()


def pair_up(block, where, axis):
    shape = list(block.shape)
    shape[axis] *= 2
    return pl.pallas_call(
        lambda *refs: pair_kernel(axis, *refs),
        out_shape=jax.ShapeDtypeStruct(shape, block.dtype),
        in_specs=[SCALARS] + [ANY] * 2,
        out_specs=ANY,
        scratch_shapes=[pltpu.SemaphoreType.DMA((2,))],
        compiler_params=PARAMS,
        cost_estimate=CHEAP,
    )(where, block, shifted(block, ZL, 1))


def prepare_kernel(tokens, out_grads, joined, turned):
    n = tokens.shape[1]
    joined[:, :n] = tokens[...]
    joined[:, n:] = out_grads[...]
    turned[:n, :] = tokens[...].T
    turned[n:, :] = out_grads[...].T


def prepare(tokens, out_grads):
    rows, k = tokens.shape[0], tokens.shape[1] + out_grads.shape[1]
    return pl.pallas_call(
        prepare_kernel,
        out_shape=[
            jax.ShapeDtypeStruct((rows, k), tokens.dtype),
            jax.ShapeDtypeStruct((k, rows), tokens.dtype),
        ],
        compiler_params=PARAMS,
        cost_estimate=CHEAP,
    )(tokens, out_grads)


def in_order(first, *later):
    return lax.optimization_barrier((first, *later))[1:]


def body(tokens, out_grads, basis_act, basis_grad):
    where = jnp.stack([lax.axis_index(axis) for axis in AXES]).astype(jnp.int32)
    joined, turned = prepare(tokens, out_grads)
    block = lax.ppermute(joined, AXES, permutation(to_group))
    (turned,) = in_order(block, turned)
    own = direct(turned, Y)
    near = gather_near(block, where, False, own[1:])
    stack = stack_up(where, own)
    stack, near = lax.optimization_barrier((stack, near))
    stacks = (stack, shifted(stack, ZL, 1))
    panel = gather_far(near, where, stacks[1])
    *parts, act_kept, act_sent = rotate(where, panel, basis_act, basis_grad, stacks)
    cov_act, cov_grad, done = covariance(where, panel, stacks)
    split, sq_act = act_squares(act_kept, act_sent)
    sq_grad = grad_squares(*sum_over_y(parts, where, (done, split)))
    block = lax.ppermute(sq_act, AXES, permutation(to_group))
    pair = pair_up(sq_grad, where, 0)
    pair, block = lax.optimization_barrier((pair, block))
    squares_own = direct(pair, Y)
    squares = gather_far(gather_near(block, where, True, squares_own[1:3]))
    correction = correct(where, squares, squares_own)
    return (cov_act, cov_grad, correction)


def solution(mesh):
    fine = Mesh(mesh.devices.reshape(SIZES), AXES)
    dp, tensor = ("zl", "y"), ("x", "zh", "c")
    placed = P(dp, tensor)
    return jax.shard_map(
        body,
        mesh=fine,
        in_specs=(placed,) * 4,
        out_specs=(P(tensor, dp), P(tensor, dp), placed),
        check_vma=False,
    )
```

```python
import itertools

import jax
import jax.numpy as jnp
from jax import lax
from jax.experimental import pallas as pl
from jax.experimental.pallas import tpu as pltpu
from jax.sharding import Mesh, PartitionSpec as P

AXES = ("zl", "y", "x", "zh", "c")
SIZES = (2, 4, 4, 4, 2)
ZL, Y, X, ZH, C = range(5)
STEPS = (0, 1, -1, 2)
ANY = pl.BlockSpec(memory_space=pl.ANY)
WHOLE = pl.BlockSpec(memory_space=pltpu.VMEM)
SCALARS = pl.BlockSpec(memory_space=pltpu.SMEM)
PARAMS = pltpu.CompilerParams(vmem_limit_bytes=48 * 1024 * 1024)

CHEAP = pl.CostEstimate(flops=1000, bytes_accessed=1000, transcendentals=0)
LONG = pl.CostEstimate(flops=5 * 10**9, bytes_accessed=20 * 10**6, transcendentals=0)


def device_index(q):
    index = 0
    for size, value in zip(SIZES, q):
        index = index * size + value
    return index


def permutation(target):
    every = itertools.product(*(range(size) for size in SIZES))
    return [(device_index(q), device_index(target(*q))) for q in every]


def shifted(value, axis, step):
    def target(*q):
        q = list(q)
        q[axis] = (q[axis] + step) % SIZES[axis]
        return q

    return lax.ppermute(value, AXES, permutation(target))


def direct(value, axis):
    return [value if step == 0 else shifted(value, axis, step) for step in STEPS]


def folded(value):
    def target(zl, y, x, zh, c):
        return zl, y, (x - 1 + 2 * c) % SIZES[X], zh, c

    return lax.ppermute(value, AXES, permutation(target))


def to_group(zl, y, x, zh, c):
    row = (x & 1) * 2 + (zh >> 1)
    flip = zl ^ (x >> 1)
    return x >> 1, row, x ^ y ^ row, ((zh >> 1) ^ flip) * 2 + ((zh & 1) ^ flip), c


def x_slot(where, step):
    return ((where[X] - step) & 3) ^ (where[ZL] * 2 + (where[Y] >> 1)) ^ where[Y]


def y_slot(where, step):
    return (where[Y] - step) & 3


def z_slot(where, step):
    slot = (where[ZH] - step) & 3
    flip = (slot >> 1) ^ (where[Y] & 1)
    return flip ^ where[ZL], (slot & 1) ^ flip


def near_kernel(turned, where, *refs):
    pieces, near, sems = refs[:4], refs[-2], refs[-1]
    copies = []
    for i, (step, piece) in enumerate(zip(STEPS, pieces)):
        zl, h = z_slot(where, step)
        tokens = piece.shape[1 if turned else 0]
        span = pl.ds(pl.multiple_of(zl * tokens, tokens), tokens)
        target = near.at[h, :, span] if turned else near.at[h, span, :]
        copies.append(pltpu.make_async_copy(piece, target, sems.at[i]))
        copies[-1].start()
    for copy in copies:
        copy.wait()


def gather_near(block, where, turned, after):
    rows, columns = block.shape
    shape = (2, rows, 2 * columns) if turned else (2, 2 * rows, columns)
    return pl.pallas_call(
        lambda *refs: near_kernel(turned, *refs),
        out_shape=jax.ShapeDtypeStruct(shape, block.dtype),
        in_specs=[SCALARS] + [ANY] * (4 + len(after)),
        out_specs=ANY,
        scratch_shapes=[pltpu.SemaphoreType.DMA((4,))],
        compiler_params=PARAMS,
        cost_estimate=CHEAP,
    )(where, *direct(block, ZH), *after)


def stack_kernel(where, *refs):
    *pieces, stack, sems = refs
    copies = []
    for i, (step, piece) in enumerate(zip(STEPS, pieces)):
        copies.append(pltpu.make_async_copy(piece, stack.at[y_slot(where, step)], sems.at[i]))
        copies[-1].start()
    for copy in copies:
        copy.wait()


def stack_up(where, pieces):
    return pl.pallas_call(
        stack_kernel,
        out_shape=jax.ShapeDtypeStruct((4,) + pieces[0].shape, pieces[0].dtype),
        in_specs=[SCALARS] + [ANY] * 4,
        out_specs=ANY,
        scratch_shapes=[pltpu.SemaphoreType.DMA((4,))],
        compiler_params=PARAMS,
        cost_estimate=CHEAP,
    )(where, *pieces)


def gather_far(near):
    own = direct(near, X)
    return own + [shifted(piece, C, 1) for piece in own]


def relay(where, left, right):
    return folded(jnp.where(where[C] == 0, right, left))


def fetch(where, pieces, panel, sems):
    copies = []
    for i, step in enumerate(STEPS):
        for j in range(2):
            copies.append(
                pltpu.make_async_copy(
                    pieces[i + 4 * j],
                    panel.at[where[C] ^ j, x_slot(where, step)],
                    sems.at[i, j],
                )
            )
            copies[-1].start()
    return copies


def dot(a, b):
    return jnp.dot(a, b, preferred_element_type=jnp.float32)


def encode(value, out):
    rows, n = value.shape
    top = jnp.max(jnp.max(jnp.abs(value), axis=0, keepdims=True), axis=1, keepdims=True)
    top = jnp.maximum(top, 1e-30).astype(jnp.bfloat16)
    power = value * (32768.0 / top.astype(jnp.float32))
    sign = power < 0
    for _ in range(3):
        power = power * power
    out[:rows, :] = jnp.where(sign, -power, power).astype(jnp.bfloat16)
    out[rows:, :] = jnp.broadcast_to(top, (16, n))


def decode(coded):
    rows = coded.shape[0] - 16
    power = coded[:rows, :].astype(jnp.float32)
    top = coded[rows:rows + 1, :].astype(jnp.float32) * (1.0 / 32768.0)
    root = jnp.abs(power)
    for _ in range(3):
        root = jnp.sqrt(root)
    return jnp.where(power < 0, -root, root) * top


def product(panel, basis, low, k):
    total = None
    for h in range(2):
        for c in range(2):
            rows = basis[(2 * h + c) * k:(2 * h + c + 1) * k, :]
            term = dot(panel(h, c)[:, low:low + k], rows)
            total = term if total is None else total + term
    return total


def rotate_some_kernel(where, *refs):
    pieces, (act_ref, grad_ref) = refs[:6], refs[6:8]
    grad_full, grad_coded, act_kept, act_sent, token = refs[-11:-6]
    panel, act, grad, held, in_sems, basis_sems = refs[-6:]
    token[...] = jnp.zeros_like(token)
    n = act.shape[1]
    copies = [
        pltpu.make_async_copy(act_ref, act, basis_sems.at[0]),
        pltpu.make_async_copy(grad_ref, grad, basis_sems.at[1]),
    ]
    for i in range(3):
        for j in range(2):
            copies.append(
                pltpu.make_async_copy(
                    pieces[i + 3 * j], panel.at[where[C] ^ j, i], in_sems.at[i, j]
                )
            )
    for copy in copies:
        copy.start()
    for copy in copies:
        copy.wait()
    rows = act_kept.shape[1]
    for i in range(3):
        total = product(lambda h, c: panel[c, i, h], grad, n, 2 * n)
        grad_full[i] = total
        encode(total, grad_coded.at[i])
        total = product(lambda h, c: panel[c, i, h], act, 0, n)
        held[0] = total[:rows]
        held[1] = total[rows:]
        act_kept[i] = held[where[ZL]]
        encode(held[1 - where[ZL]], act_sent.at[i])


def rotate_some(where, pieces, basis_act, basis_grad):
    rows, k = pieces[0].shape[1:]
    n = k // 3
    f32, bf16 = jnp.float32, jnp.bfloat16
    return pl.pallas_call(
        rotate_some_kernel,
        out_shape=[
            jax.ShapeDtypeStruct((3, rows, 2 * n), f32),
            jax.ShapeDtypeStruct((3, rows + 16, 2 * n), bf16),
            jax.ShapeDtypeStruct((3, rows // 2, n), f32),
            jax.ShapeDtypeStruct((3, rows // 2 + 16, n), bf16),
            jax.ShapeDtypeStruct((8, 128), f32),
        ],
        in_specs=[SCALARS] + [ANY] * 8,
        scratch_shapes=[
            pltpu.VMEM((2, 3, 2, rows, k), bf16),
            pltpu.VMEM(basis_act.shape, bf16),
            pltpu.VMEM(basis_grad.shape, bf16),
            pltpu.VMEM((2, rows // 2, n), f32),
            pltpu.SemaphoreType.DMA((3, 2)),
            pltpu.SemaphoreType.DMA((2,)),
        ],
        compiler_params=PARAMS,
        cost_estimate=LONG,
    )(where, *pieces, basis_act, basis_grad)


def rotate_last_kernel(where, *refs):
    pieces, (act_ref, grad_ref), done = refs[:2], refs[2:4], refs[4:8]
    outs, act_kept, act_sent = refs[8:12], refs[12], refs[13]
    panel, act, grad, held, grad_full, grad_coded, kept, sent, in_sems, out_sems = refs[14:]
    n = act.shape[1]
    copies = [
        pltpu.make_async_copy(act_ref, act, in_sems.at[0]),
        pltpu.make_async_copy(grad_ref, grad, in_sems.at[1]),
    ]
    for j in range(2):
        copies.append(
            pltpu.make_async_copy(pieces[j], panel.at[where[C] ^ j], in_sems.at[2 + j])
        )
    for copy in copies:
        copy.start()

    def route(i, step, sources, act_on):
        due = (x_slot(where, step) - where[Y]) & 3
        for j, y_step in enumerate(STEPS):
            @pl.when(due == (y_step & 3))
            def _():
                source = sources[0] if j == 0 else sources[1]
                for copy in (
                    pltpu.make_async_copy(source, outs[j], out_sems.at[i, 0]),
                    pltpu.make_async_copy(sources[2], act_kept.at[j], out_sems.at[i, 1]),
                    pltpu.make_async_copy(sources[3], act_sent.at[j], out_sems.at[i, 2]),
                ):
                    act_on(copy)

    parts = [(i, STEPS[i], [ref.at[i] for ref in done]) for i in range(3)]
    for part in parts:
        route(*part, lambda copy: copy.start())
    for copy in copies:
        copy.wait()
    rows = kept.shape[0]
    total = product(lambda h, c: panel[c, h], grad, n, 2 * n)
    grad_full[...] = total
    encode(total, grad_coded)
    total = product(lambda h, c: panel[c, h], act, 0, n)
    held[0] = total[:rows]
    held[1] = total[rows:]
    kept[...] = held[where[ZL]]
    encode(held[1 - where[ZL]], sent)
    parts.append((3, STEPS[3], [grad_full, grad_coded, kept, sent]))
    route(*parts[3], lambda copy: copy.start())
    for part in parts:
        route(*part, lambda copy: copy.wait())


def rotate_last(where, pieces, basis_act, basis_grad, done):
    rows, k = pieces[0].shape[1:]
    n = k // 3
    f32, bf16 = jnp.float32, jnp.bfloat16
    return pl.pallas_call(
        rotate_last_kernel,
        out_shape=[jax.ShapeDtypeStruct((rows, 2 * n), f32)]
        + [jax.ShapeDtypeStruct((rows + 16, 2 * n), bf16)] * 3
        + [
            jax.ShapeDtypeStruct((4, rows // 2, n), f32),
            jax.ShapeDtypeStruct((4, rows // 2 + 16, n), bf16),
        ],
        in_specs=[SCALARS] + [ANY] * 8,
        out_specs=[ANY] * 6,
        scratch_shapes=[
            pltpu.VMEM((2, 2, rows, k), bf16),
            pltpu.VMEM(basis_act.shape, bf16),
            pltpu.VMEM(basis_grad.shape, bf16),
            pltpu.VMEM((2, rows // 2, n), f32),
            pltpu.VMEM((rows, 2 * n), f32),
            pltpu.VMEM((rows + 16, 2 * n), bf16),
            pltpu.VMEM((rows // 2, n), f32),
            pltpu.VMEM((rows // 2 + 16, n), bf16),
            pltpu.SemaphoreType.DMA((4,)),
            pltpu.SemaphoreType.DMA((4, 3)),
        ],
        compiler_params=PARAMS,
        cost_estimate=CHEAP,
    )(where, *pieces, basis_act, basis_grad, *done)


def covariance_kernel(where, *refs):
    pieces, stacks, outs, token = refs[:8], refs[8:10], refs[10:12], refs[12]
    panel, own, act, grad, in_sems, own_sems, out_sems = refs[13:]
    token[...] = jnp.zeros_like(token)
    n = act.shape[1]
    rows = stacks[0].shape[2]
    tokens = 2 * rows
    copies = []
    for i, stack in enumerate(stacks):
        for y in range(4):
            start = pl.multiple_of((2 * y + (where[ZL] ^ i)) * rows, rows)
            copies.append(
                pltpu.make_async_copy(stack.at[y], own.at[:, pl.ds(start, rows)], own_sems.at[i, y])
            )
            copies[-1].start()
    copies += fetch(where, pieces, panel, in_sems)
    for copy in copies:
        copy.wait()
    scale = 1.0 / (4 * tokens)
    waits = []
    for h in range(2):
        for c in range(2):
            block = 2 * h + c
            for j, (held, out, low, k) in enumerate(((act, outs[0], 0, n), (grad, outs[1], n, 2 * n))):
                total = None
                for y in range(4):
                    term = dot(
                        own[low:low + k, y * tokens:(y + 1) * tokens],
                        panel[c, y, h, :, low:low + k],
                    )
                    total = term if total is None else total + term
                held[block] = total * scale
                waits.append(
                    pltpu.make_async_copy(
                        held.at[block], out.at[:, block * k:(block + 1) * k], out_sems.at[block, j]
                    )
                )
                waits[-1].start()
    for copy in waits:
        copy.wait()


def covariance(where, pieces, mine):
    rows, k = pieces[0].shape[1:]
    n = k // 3
    f32, bf16 = jnp.float32, jnp.bfloat16
    return pl.pallas_call(
        covariance_kernel,
        out_shape=[
            jax.ShapeDtypeStruct((n, 4 * n), f32),
            jax.ShapeDtypeStruct((2 * n, 8 * n), f32),
            jax.ShapeDtypeStruct((8, 128), f32),
        ],
        in_specs=[SCALARS] + [ANY] * 10,
        out_specs=[ANY] * 2 + [WHOLE],
        scratch_shapes=[
            pltpu.VMEM((2, 4, 2, rows, k), bf16),
            pltpu.VMEM((k, 4 * rows), bf16),
            pltpu.VMEM((4, n, n), f32),
            pltpu.VMEM((4, 2 * n, 2 * n), f32),
            pltpu.SemaphoreType.DMA((4, 2)),
            pltpu.SemaphoreType.DMA((2, 4)),
            pltpu.SemaphoreType.DMA((4, 2)),
        ],
        compiler_params=PARAMS,
        cost_estimate=LONG,
    )(where, *pieces, *mine)


def correction_kernel(where, *refs):
    pieces, squares, out = refs[:8], refs[8:12], refs[12]
    panel, grad, held, in_sems, grad_sems, out_sems = refs[13:]
    rows, tokens = panel.shape[3:]
    copies = fetch(where, pieces, panel, in_sems)
    for i, step in enumerate(STEPS):
        copies.append(
            pltpu.make_async_copy(squares[i], grad.at[y_slot(where, step)], grad_sems.at[i])
        )
        copies[-1].start()
    for copy in copies:
        copy.wait()
    scale = 1.0 / (4 * tokens)
    waits = []
    for h in range(2):
        for c in range(2):
            block = 2 * h + c
            total = None
            for y in range(4):
                term = dot(panel[c, y, h], grad[y])
                total = term if total is None else total + term
            held[block] = total * scale
            waits.append(
                pltpu.make_async_copy(
                    held.at[block], out.at[block * rows:(block + 1) * rows, :], out_sems.at[block]
                )
            )
            waits[-1].start()
    for copy in waits:
        copy.wait()


def correct(where, pieces, squares):
    rows, tokens = pieces[0].shape[1:]
    n = squares[0].shape[1]
    f32, bf16 = jnp.float32, jnp.bfloat16
    return pl.pallas_call(
        correction_kernel,
        out_shape=jax.ShapeDtypeStruct((4 * rows, n), f32),
        in_specs=[SCALARS] + [ANY] * 12,
        out_specs=ANY,
        scratch_shapes=[
            pltpu.VMEM((2, 4, 2, rows, tokens), bf16),
            pltpu.VMEM((4, tokens, n), bf16),
            pltpu.VMEM((4, rows, n), f32),
            pltpu.SemaphoreType.DMA((4, 2)),
            pltpu.SemaphoreType.DMA((4,)),
            pltpu.SemaphoreType.DMA((4,)),
        ],
        compiler_params=PARAMS,
        cost_estimate=CHEAP,
    )(where, *pieces, *squares)


def half_kernel(where, own, *refs):
    arrived, kept, sent, total = refs[:3], refs[-3], refs[-2], refs[-1]
    rows = kept.shape[0]
    whole = own[...]
    for coded in arrived:
        whole = whole + decode(coded)
    for i in range(2):
        total[i] = whole[i * rows:(i + 1) * rows]
    kept[...] = total[where[ZL]]
    encode(total[1 - where[ZL]], sent)


def sum_over_y(parts, where, after=()):
    rows, n = parts[0].shape
    rows = rows // 2
    parts = [part if step == 0 else shifted(part, Y, step) for step, part in zip(STEPS, parts)]
    return pl.pallas_call(
        half_kernel,
        out_shape=[
            jax.ShapeDtypeStruct((rows, n), jnp.float32),
            jax.ShapeDtypeStruct((rows + 16, n), jnp.bfloat16),
        ],
        in_specs=[SCALARS] + [WHOLE] * 4 + [ANY] * len(after),
        scratch_shapes=[pltpu.VMEM((2, rows, n), jnp.float32)],
        compiler_params=PARAMS,
        cost_estimate=CHEAP,
    )(where, *parts, *after)


def grad_square_kernel(kept, arrived, out):
    total = kept[...] + decode(arrived)
    out[...] = (total * total).astype(jnp.bfloat16)


def grad_squares(kept, sent):
    return pl.pallas_call(
        grad_square_kernel,
        out_shape=jax.ShapeDtypeStruct(kept.shape, jnp.bfloat16),
        compiler_params=PARAMS,
        cost_estimate=CHEAP,
    )(kept, shifted(sent, ZL, 1))


def split_kernel(kept, arrived, *outs):
    rows, n = kept.shape[1:]
    outs[0][...] = kept[0] + decode(arrived.at[0])
    for i in range(1, 4):
        encode(kept[i] + decode(arrived.at[i]), outs[i])


def act_square_kernel(own, *refs):
    total = own[...]
    for coded in refs[:3]:
        total = total + decode(coded)
    refs[3][...] = (total * total).T.astype(jnp.bfloat16)


def act_squares(kept, sent):
    rows, n = kept.shape[1:]
    parts = pl.pallas_call(
        split_kernel,
        out_shape=[jax.ShapeDtypeStruct((rows, n), jnp.float32)]
        + [jax.ShapeDtypeStruct((rows + 16, n), jnp.bfloat16)] * 3,
        compiler_params=PARAMS,
        cost_estimate=CHEAP,
    )(kept, shifted(sent, ZL, 1))
    return parts[0], pl.pallas_call(
        act_square_kernel,
        out_shape=jax.ShapeDtypeStruct((n, rows), jnp.bfloat16),
        compiler_params=PARAMS,
        cost_estimate=CHEAP,
    )(*[part if step == 0 else shifted(part, Y, step) for step, part in zip(STEPS, parts)])


def pair_kernel(axis, where, own, other, pair, sems):
    size = own.shape[axis]
    copies = []
    for i, (ref, zl) in enumerate(((own, where[ZL]), (other, 1 - where[ZL]))):
        span = pl.ds(pl.multiple_of(zl * size, size), size)
        target = pair.at[:, span] if axis else pair.at[span, :]
        copies.append(pltpu.make_async_copy(ref, target, sems.at[i]))
        copies[-1].start()
    for copy in copies:
        copy.wait()


def pair_up(block, where, axis):
    shape = list(block.shape)
    shape[axis] *= 2
    return pl.pallas_call(
        lambda *refs: pair_kernel(axis, *refs),
        out_shape=jax.ShapeDtypeStruct(shape, block.dtype),
        in_specs=[SCALARS] + [ANY] * 2,
        out_specs=ANY,
        scratch_shapes=[pltpu.SemaphoreType.DMA((2,))],
        compiler_params=PARAMS,
        cost_estimate=CHEAP,
    )(where, block, shifted(block, ZL, 1))


def prepare_kernel(tokens, out_grads, joined, turned):
    n = tokens.shape[1]
    joined[:, :n] = tokens[...]
    joined[:, n:] = out_grads[...]
    turned[:n, :] = tokens[...].T
    turned[n:, :] = out_grads[...].T


def prepare(tokens, out_grads):
    rows, k = tokens.shape[0], tokens.shape[1] + out_grads.shape[1]
    return pl.pallas_call(
        prepare_kernel,
        out_shape=[
            jax.ShapeDtypeStruct((rows, k), tokens.dtype),
            jax.ShapeDtypeStruct((k, rows), tokens.dtype),
        ],
        compiler_params=PARAMS,
        cost_estimate=CHEAP,
    )(tokens, out_grads)


def in_order(first, *later):
    return lax.optimization_barrier((first, *later))[1:]


def pass_kernel(value, after, out, sem):
    copy = pltpu.make_async_copy(value, out, sem)
    copy.start()
    copy.wait()


def pass_on(value, after):
    return pl.pallas_call(
        pass_kernel,
        out_shape=jax.ShapeDtypeStruct(value.shape, value.dtype),
        in_specs=[ANY] * 2,
        out_specs=ANY,
        scratch_shapes=[pltpu.SemaphoreType.DMA],
        compiler_params=PARAMS,
        cost_estimate=CHEAP,
    )(value, after)


def body(tokens, out_grads, basis_act, basis_grad):
    where = jnp.stack([lax.axis_index(axis) for axis in AXES]).astype(jnp.int32)
    joined, turned = prepare(tokens, out_grads)
    block = lax.ppermute(joined, AXES, permutation(to_group))
    (turned,) = in_order(block, turned)
    own = direct(turned, Y)
    near = gather_near(block, where, False, own[1:])
    stack = stack_up(where, own)
    stack, near = lax.optimization_barrier((stack, near))
    stacks = (stack, shifted(stack, ZL, 1))
    left, right = shifted(near, X, 1), shifted(near, X, -1)
    own = [near, left, right]
    _, left, right = lax.optimization_barrier((stacks[1], left, right))
    far = relay(where, left, right)
    other = [shifted(piece, C, 1) for piece in own]
    *some, token = rotate_some(where, own + other, basis_act, basis_grad)
    last = [far, shifted(pass_on(far, token), C, 1)]
    panel = own + last[:1] + other + last[1:]
    *parts, act_kept, act_sent = rotate_last(where, last, basis_act, basis_grad, some)
    cov_act, cov_grad, done = covariance(where, panel, stacks)
    split, sq_act = act_squares(act_kept, act_sent)
    sq_grad = grad_squares(*sum_over_y(parts, where, (split,)))
    block = lax.ppermute(sq_act, AXES, permutation(to_group))
    pair = pair_up(sq_grad, where, 0)
    pair, block = lax.optimization_barrier((pair, block))
    squares_own = direct(pair, Y)
    squares = gather_far(gather_near(block, where, True, squares_own[1:3] + [done]))
    correction = correct(where, squares, squares_own)
    return (cov_act, cov_grad, correction)


def solution(mesh):
    fine = Mesh(mesh.devices.reshape(SIZES), AXES)
    dp, tensor = ("zl", "y"), ("x", "zh", "c")
    placed = P(dp, tensor)
    return jax.shard_map(
        body,
        mesh=fine,
        in_specs=(placed,) * 4,
        out_specs=(P(tensor, dp), P(tensor, dp), placed),
        check_vma=False,
    )
```

```python
import itertools

import jax
import jax.numpy as jnp
from jax import lax
from jax.experimental import pallas as pl
from jax.experimental.pallas import tpu as pltpu
from jax.sharding import Mesh, PartitionSpec as P

AXES = ("zl", "y", "x", "zh", "c")
SIZES = (2, 4, 4, 4, 2)
ZL, Y, X, ZH, C = range(5)
STEPS = (0, 1, -1, 2)
ANY = pl.BlockSpec(memory_space=pl.ANY)
WHOLE = pl.BlockSpec(memory_space=pltpu.VMEM)
SCALARS = pl.BlockSpec(memory_space=pltpu.SMEM)
PARAMS = pltpu.CompilerParams(vmem_limit_bytes=48 * 1024 * 1024)

CHEAP = pl.CostEstimate(flops=1000, bytes_accessed=1000, transcendentals=0)
LONG = pl.CostEstimate(flops=5 * 10**9, bytes_accessed=20 * 10**6, transcendentals=0)


def device_index(q):
    index = 0
    for size, value in zip(SIZES, q):
        index = index * size + value
    return index


def permutation(target):
    every = itertools.product(*(range(size) for size in SIZES))
    return [(device_index(q), device_index(target(*q))) for q in every]


def shifted(value, axis, step):
    def target(*q):
        q = list(q)
        q[axis] = (q[axis] + step) % SIZES[axis]
        return q

    return lax.ppermute(value, AXES, permutation(target))


def direct(value, axis):
    return [value if step == 0 else shifted(value, axis, step) for step in STEPS]


def folded(value):
    def target(zl, y, x, zh, c):
        return zl, y, (x - 1 + 2 * c) % SIZES[X], zh, c

    return lax.ppermute(value, AXES, permutation(target))


def to_group(zl, y, x, zh, c):
    row = (x & 1) * 2 + (zh >> 1)
    flip = zl ^ (x >> 1)
    return x >> 1, row, x ^ y ^ row, ((zh >> 1) ^ flip) * 2 + ((zh & 1) ^ flip), c


def x_slot(where, step):
    return ((where[X] - step) & 3) ^ (where[ZL] * 2 + (where[Y] >> 1)) ^ where[Y]


def y_slot(where, step):
    return (where[Y] - step) & 3


def z_slot(where, step):
    slot = (where[ZH] - step) & 3
    flip = (slot >> 1) ^ (where[Y] & 1)
    return flip ^ where[ZL], (slot & 1) ^ flip


def near_kernel(turned, where, *refs):
    pieces, near, sems = refs[:4], refs[-2], refs[-1]
    copies = []
    for i, (step, piece) in enumerate(zip(STEPS, pieces)):
        zl, h = z_slot(where, step)
        tokens = piece.shape[1 if turned else 0]
        span = pl.ds(pl.multiple_of(zl * tokens, tokens), tokens)
        target = near.at[h, :, span] if turned else near.at[h, span, :]
        copies.append(pltpu.make_async_copy(piece, target, sems.at[i]))
        copies[-1].start()
    for copy in copies:
        copy.wait()


def gather_near(block, where, turned, after):
    rows, columns = block.shape
    shape = (2, rows, 2 * columns) if turned else (2, 2 * rows, columns)
    return pl.pallas_call(
        lambda *refs: near_kernel(turned, *refs),
        out_shape=jax.ShapeDtypeStruct(shape, block.dtype),
        in_specs=[SCALARS] + [ANY] * (4 + len(after)),
        out_specs=ANY,
        scratch_shapes=[pltpu.SemaphoreType.DMA((4,))],
        compiler_params=PARAMS,
        cost_estimate=CHEAP,
    )(where, *direct(block, ZH), *after)


def stack_kernel(where, *refs):
    *pieces, stack, sems = refs
    copies = []
    for i, (step, piece) in enumerate(zip(STEPS, pieces)):
        copies.append(pltpu.make_async_copy(piece, stack.at[y_slot(where, step)], sems.at[i]))
        copies[-1].start()
    for copy in copies:
        copy.wait()


def stack_up(where, pieces):
    return pl.pallas_call(
        stack_kernel,
        out_shape=jax.ShapeDtypeStruct((4,) + pieces[0].shape, pieces[0].dtype),
        in_specs=[SCALARS] + [ANY] * 4,
        out_specs=ANY,
        scratch_shapes=[pltpu.SemaphoreType.DMA((4,))],
        compiler_params=PARAMS,
        cost_estimate=CHEAP,
    )(where, *pieces)


def gather_far(near):
    own = direct(near, X)
    return own + [shifted(piece, C, 1) for piece in own]


def relay(where, left, right):
    return folded(jnp.where(where[C] == 0, right, left))


def fetch(where, pieces, panel, sems):
    copies = []
    for i, step in enumerate(STEPS):
        for j in range(2):
            copies.append(
                pltpu.make_async_copy(
                    pieces[i + 4 * j],
                    panel.at[where[C] ^ j, x_slot(where, step)],
                    sems.at[i, j],
                )
            )
            copies[-1].start()
    return copies


def dot(a, b):
    return jnp.dot(a, b, preferred_element_type=jnp.float32)


def encode(value, out):
    rows, n = value.shape
    top = jnp.max(jnp.max(jnp.abs(value), axis=0, keepdims=True), axis=1, keepdims=True)
    top = jnp.maximum(top, 1e-30).astype(jnp.bfloat16)
    power = value * (32768.0 / top.astype(jnp.float32))
    sign = power < 0
    for _ in range(3):
        power = power * power
    out[:rows, :] = jnp.where(sign, -power, power).astype(jnp.bfloat16)
    out[rows:, :] = jnp.broadcast_to(top, (16, n))


def decode(coded):
    rows = coded.shape[0] - 16
    power = coded[:rows, :].astype(jnp.float32)
    top = coded[rows:rows + 1, :].astype(jnp.float32) * (1.0 / 32768.0)
    root = jnp.abs(power)
    for _ in range(3):
        root = jnp.sqrt(root)
    return jnp.where(power < 0, -root, root) * top


def product(panel, basis, low, k):
    total = None
    for h in range(2):
        for c in range(2):
            rows = basis[(2 * h + c) * k:(2 * h + c + 1) * k, :]
            term = dot(panel(h, c)[:, low:low + k], rows)
            total = term if total is None else total + term
    return total


def rotate_some_kernel(where, *refs):
    pieces, (act_ref, grad_ref) = refs[:6], refs[6:8]
    grad_full, grad_coded, act_kept, act_sent, token = refs[-11:-6]
    panel, act, grad, held, in_sems, basis_sems = refs[-6:]
    token[...] = jnp.zeros_like(token)
    n = act.shape[1]
    copies = [
        pltpu.make_async_copy(act_ref, act, basis_sems.at[0]),
        pltpu.make_async_copy(grad_ref, grad, basis_sems.at[1]),
    ]
    for i in range(3):
        for j in range(2):
            copies.append(
                pltpu.make_async_copy(
                    pieces[i + 3 * j], panel.at[where[C] ^ j, i], in_sems.at[i, j]
                )
            )
    for copy in copies:
        copy.start()
    for copy in copies:
        copy.wait()
    rows = act_kept.shape[1]
    for i in range(3):
        total = product(lambda h, c: panel[c, i, h], grad, n, 2 * n)
        grad_full[i] = total
        encode(total, grad_coded.at[i])
        total = product(lambda h, c: panel[c, i, h], act, 0, n)
        held[0] = total[:rows]
        held[1] = total[rows:]
        act_kept[i] = held[where[ZL]]
        encode(held[1 - where[ZL]], act_sent.at[i])


def rotate_some(where, pieces, basis_act, basis_grad, after):
    rows, k = pieces[0].shape[1:]
    n = k // 3
    f32, bf16 = jnp.float32, jnp.bfloat16
    return pl.pallas_call(
        rotate_some_kernel,
        out_shape=[
            jax.ShapeDtypeStruct((3, rows, 2 * n), f32),
            jax.ShapeDtypeStruct((3, rows + 16, 2 * n), bf16),
            jax.ShapeDtypeStruct((3, rows // 2, n), f32),
            jax.ShapeDtypeStruct((3, rows // 2 + 16, n), bf16),
            jax.ShapeDtypeStruct((8, 128), f32),
        ],
        in_specs=[SCALARS] + [ANY] * 9,
        scratch_shapes=[
            pltpu.VMEM((2, 3, 2, rows, k), bf16),
            pltpu.VMEM(basis_act.shape, bf16),
            pltpu.VMEM(basis_grad.shape, bf16),
            pltpu.VMEM((2, rows // 2, n), f32),
            pltpu.SemaphoreType.DMA((3, 2)),
            pltpu.SemaphoreType.DMA((2,)),
        ],
        compiler_params=PARAMS,
        cost_estimate=LONG,
    )(where, *pieces, basis_act, basis_grad, after)


def rotate_last_kernel(where, *refs):
    pieces, (act_ref, grad_ref), done = refs[:2], refs[2:4], refs[4:8]
    outs, act_kept, act_sent = refs[8:12], refs[12], refs[13]
    panel, act, grad, held, grad_full, grad_coded, kept, sent, in_sems, out_sems = refs[14:]
    n = act.shape[1]
    copies = [
        pltpu.make_async_copy(act_ref, act, in_sems.at[0]),
        pltpu.make_async_copy(grad_ref, grad, in_sems.at[1]),
    ]
    for j in range(2):
        copies.append(
            pltpu.make_async_copy(pieces[j], panel.at[where[C] ^ j], in_sems.at[2 + j])
        )
    for copy in copies:
        copy.start()

    def route(i, step, sources, act_on):
        due = (x_slot(where, step) - where[Y]) & 3
        for j, y_step in enumerate(STEPS):
            @pl.when(due == (y_step & 3))
            def _():
                source = sources[0] if j == 0 else sources[1]
                for copy in (
                    pltpu.make_async_copy(source, outs[j], out_sems.at[i, 0]),
                    pltpu.make_async_copy(sources[2], act_kept.at[j], out_sems.at[i, 1]),
                    pltpu.make_async_copy(sources[3], act_sent.at[j], out_sems.at[i, 2]),
                ):
                    act_on(copy)

    parts = [(i, STEPS[i], [ref.at[i] for ref in done]) for i in range(3)]
    for part in parts:
        route(*part, lambda copy: copy.start())
    for copy in copies:
        copy.wait()
    rows = kept.shape[0]
    total = product(lambda h, c: panel[c, h], grad, n, 2 * n)
    grad_full[...] = total
    encode(total, grad_coded)
    total = product(lambda h, c: panel[c, h], act, 0, n)
    held[0] = total[:rows]
    held[1] = total[rows:]
    kept[...] = held[where[ZL]]
    encode(held[1 - where[ZL]], sent)
    parts.append((3, STEPS[3], [grad_full, grad_coded, kept, sent]))
    route(*parts[3], lambda copy: copy.start())
    for part in parts:
        route(*part, lambda copy: copy.wait())


def rotate_last(where, pieces, basis_act, basis_grad, done):
    rows, k = pieces[0].shape[1:]
    n = k // 3
    f32, bf16 = jnp.float32, jnp.bfloat16
    return pl.pallas_call(
        rotate_last_kernel,
        out_shape=[jax.ShapeDtypeStruct((rows, 2 * n), f32)]
        + [jax.ShapeDtypeStruct((rows + 16, 2 * n), bf16)] * 3
        + [
            jax.ShapeDtypeStruct((4, rows // 2, n), f32),
            jax.ShapeDtypeStruct((4, rows // 2 + 16, n), bf16),
        ],
        in_specs=[SCALARS] + [ANY] * 8,
        out_specs=[ANY] * 6,
        scratch_shapes=[
            pltpu.VMEM((2, 2, rows, k), bf16),
            pltpu.VMEM(basis_act.shape, bf16),
            pltpu.VMEM(basis_grad.shape, bf16),
            pltpu.VMEM((2, rows // 2, n), f32),
            pltpu.VMEM((rows, 2 * n), f32),
            pltpu.VMEM((rows + 16, 2 * n), bf16),
            pltpu.VMEM((rows // 2, n), f32),
            pltpu.VMEM((rows // 2 + 16, n), bf16),
            pltpu.SemaphoreType.DMA((4,)),
            pltpu.SemaphoreType.DMA((4, 3)),
        ],
        compiler_params=PARAMS,
        cost_estimate=CHEAP,
    )(where, *pieces, basis_act, basis_grad, *done)


def covariance_kernel(where, *refs):
    pieces, stacks, outs, token = refs[:8], refs[8:10], refs[10:12], refs[12]
    panel, own, act, grad, in_sems, own_sems, out_sems = refs[13:]
    token[...] = jnp.zeros_like(token)
    n = act.shape[1]
    rows = stacks[0].shape[2]
    tokens = 2 * rows
    copies = []
    for i, stack in enumerate(stacks):
        for y in range(4):
            start = pl.multiple_of((2 * y + (where[ZL] ^ i)) * rows, rows)
            copies.append(
                pltpu.make_async_copy(stack.at[y], own.at[:, pl.ds(start, rows)], own_sems.at[i, y])
            )
            copies[-1].start()
    copies += fetch(where, pieces, panel, in_sems)
    for copy in copies:
        copy.wait()
    scale = 1.0 / (4 * tokens)
    waits = []
    for h in range(2):
        for c in range(2):
            block = 2 * h + c
            for j, (held, out, low, k) in enumerate(((act, outs[0], 0, n), (grad, outs[1], n, 2 * n))):
                total = None
                for y in range(4):
                    term = dot(
                        own[low:low + k, y * tokens:(y + 1) * tokens],
                        panel[c, y, h, :, low:low + k],
                    )
                    total = term if total is None else total + term
                held[block] = total * scale
                waits.append(
                    pltpu.make_async_copy(
                        held.at[block], out.at[:, block * k:(block + 1) * k], out_sems.at[block, j]
                    )
                )
                waits[-1].start()
    for copy in waits:
        copy.wait()


def covariance(where, pieces, mine):
    rows, k = pieces[0].shape[1:]
    n = k // 3
    f32, bf16 = jnp.float32, jnp.bfloat16
    return pl.pallas_call(
        covariance_kernel,
        out_shape=[
            jax.ShapeDtypeStruct((n, 4 * n), f32),
            jax.ShapeDtypeStruct((2 * n, 8 * n), f32),
            jax.ShapeDtypeStruct((8, 128), f32),
        ],
        in_specs=[SCALARS] + [ANY] * 10,
        out_specs=[ANY] * 2 + [WHOLE],
        scratch_shapes=[
            pltpu.VMEM((2, 4, 2, rows, k), bf16),
            pltpu.VMEM((k, 4 * rows), bf16),
            pltpu.VMEM((4, n, n), f32),
            pltpu.VMEM((4, 2 * n, 2 * n), f32),
            pltpu.SemaphoreType.DMA((4, 2)),
            pltpu.SemaphoreType.DMA((2, 4)),
            pltpu.SemaphoreType.DMA((4, 2)),
        ],
        compiler_params=PARAMS,
        cost_estimate=LONG,
    )(where, *pieces, *mine)


def correction_kernel(where, *refs):
    pieces, squares, out = refs[:8], refs[8:12], refs[12]
    panel, grad, held, in_sems, grad_sems, out_sems = refs[13:]
    rows, tokens = panel.shape[3:]
    copies = fetch(where, pieces, panel, in_sems)
    for i, step in enumerate(STEPS):
        copies.append(
            pltpu.make_async_copy(squares[i], grad.at[y_slot(where, step)], grad_sems.at[i])
        )
        copies[-1].start()
    for copy in copies:
        copy.wait()
    scale = 1.0 / (4 * tokens)
    waits = []
    for h in range(2):
        for c in range(2):
            block = 2 * h + c
            total = None
            for y in range(4):
                term = dot(panel[c, y, h], grad[y])
                total = term if total is None else total + term
            held[block] = total * scale
            waits.append(
                pltpu.make_async_copy(
                    held.at[block], out.at[block * rows:(block + 1) * rows, :], out_sems.at[block]
                )
            )
            waits[-1].start()
    for copy in waits:
        copy.wait()


def correct(where, pieces, squares):
    rows, tokens = pieces[0].shape[1:]
    n = squares[0].shape[1]
    f32, bf16 = jnp.float32, jnp.bfloat16
    return pl.pallas_call(
        correction_kernel,
        out_shape=jax.ShapeDtypeStruct((4 * rows, n), f32),
        in_specs=[SCALARS] + [ANY] * 12,
        out_specs=ANY,
        scratch_shapes=[
            pltpu.VMEM((2, 4, 2, rows, tokens), bf16),
            pltpu.VMEM((4, tokens, n), bf16),
            pltpu.VMEM((4, rows, n), f32),
            pltpu.SemaphoreType.DMA((4, 2)),
            pltpu.SemaphoreType.DMA((4,)),
            pltpu.SemaphoreType.DMA((4,)),
        ],
        compiler_params=PARAMS,
        cost_estimate=CHEAP,
    )(where, *pieces, *squares)


def half_kernel(where, own, *refs):
    arrived, kept, sent, total = refs[:3], refs[-3], refs[-2], refs[-1]
    rows = kept.shape[0]
    whole = own[...]
    for coded in arrived:
        whole = whole + decode(coded)
    for i in range(2):
        total[i] = whole[i * rows:(i + 1) * rows]
    kept[...] = total[where[ZL]]
    encode(total[1 - where[ZL]], sent)


def sum_over_y(parts, where, after=()):
    rows, n = parts[0].shape
    rows = rows // 2
    parts = [part if step == 0 else shifted(part, Y, step) for step, part in zip(STEPS, parts)]
    return pl.pallas_call(
        half_kernel,
        out_shape=[
            jax.ShapeDtypeStruct((rows, n), jnp.float32),
            jax.ShapeDtypeStruct((rows + 16, n), jnp.bfloat16),
        ],
        in_specs=[SCALARS] + [WHOLE] * 4 + [ANY] * len(after),
        scratch_shapes=[pltpu.VMEM((2, rows, n), jnp.float32)],
        compiler_params=PARAMS,
        cost_estimate=CHEAP,
    )(where, *parts, *after)


def grad_square_kernel(kept, arrived, out):
    total = kept[...] + decode(arrived)
    out[...] = (total * total).astype(jnp.bfloat16)


def grad_squares(kept, sent):
    return pl.pallas_call(
        grad_square_kernel,
        out_shape=jax.ShapeDtypeStruct(kept.shape, jnp.bfloat16),
        compiler_params=PARAMS,
        cost_estimate=CHEAP,
    )(kept, shifted(sent, ZL, 1))


def split_kernel(kept, arrived, *outs):
    rows, n = kept.shape[1:]
    outs[0][...] = kept[0] + decode(arrived.at[0])
    for i in range(1, 4):
        encode(kept[i] + decode(arrived.at[i]), outs[i])


def act_square_kernel(own, *refs):
    total = own[...]
    for coded in refs[:3]:
        total = total + decode(coded)
    refs[3][...] = (total * total).T.astype(jnp.bfloat16)


def act_squares(kept, sent):
    rows, n = kept.shape[1:]
    parts = pl.pallas_call(
        split_kernel,
        out_shape=[jax.ShapeDtypeStruct((rows, n), jnp.float32)]
        + [jax.ShapeDtypeStruct((rows + 16, n), jnp.bfloat16)] * 3,
        compiler_params=PARAMS,
        cost_estimate=CHEAP,
    )(kept, shifted(sent, ZL, 1))
    return parts[0], pl.pallas_call(
        act_square_kernel,
        out_shape=jax.ShapeDtypeStruct((n, rows), jnp.bfloat16),
        compiler_params=PARAMS,
        cost_estimate=CHEAP,
    )(*[part if step == 0 else shifted(part, Y, step) for step, part in zip(STEPS, parts)])


def pair_kernel(axis, where, own, other, pair, sems):
    size = own.shape[axis]
    copies = []
    for i, (ref, zl) in enumerate(((own, where[ZL]), (other, 1 - where[ZL]))):
        span = pl.ds(pl.multiple_of(zl * size, size), size)
        target = pair.at[:, span] if axis else pair.at[span, :]
        copies.append(pltpu.make_async_copy(ref, target, sems.at[i]))
        copies[-1].start()
    for copy in copies:
        copy.wait()


def pair_up(block, where, axis):
    shape = list(block.shape)
    shape[axis] *= 2
    return pl.pallas_call(
        lambda *refs: pair_kernel(axis, *refs),
        out_shape=jax.ShapeDtypeStruct(shape, block.dtype),
        in_specs=[SCALARS] + [ANY] * 2,
        out_specs=ANY,
        scratch_shapes=[pltpu.SemaphoreType.DMA((2,))],
        compiler_params=PARAMS,
        cost_estimate=CHEAP,
    )(where, block, shifted(block, ZL, 1))


def prepare_kernel(tokens, out_grads, joined, turned):
    n = tokens.shape[1]
    joined[:, :n] = tokens[...]
    joined[:, n:] = out_grads[...]
    turned[:n, :] = tokens[...].T
    turned[n:, :] = out_grads[...].T


def prepare(tokens, out_grads):
    rows, k = tokens.shape[0], tokens.shape[1] + out_grads.shape[1]
    return pl.pallas_call(
        prepare_kernel,
        out_shape=[
            jax.ShapeDtypeStruct((rows, k), tokens.dtype),
            jax.ShapeDtypeStruct((k, rows), tokens.dtype),
        ],
        compiler_params=PARAMS,
        cost_estimate=CHEAP,
    )(tokens, out_grads)


def in_order(first, *later):
    return lax.optimization_barrier((first, *later))[1:]


def pass_kernel(value, after, out, sem):
    copy = pltpu.make_async_copy(value, out, sem)
    copy.start()
    copy.wait()


def pass_on(value, after):
    return pl.pallas_call(
        pass_kernel,
        out_shape=jax.ShapeDtypeStruct(value.shape, value.dtype),
        in_specs=[ANY] * 2,
        out_specs=ANY,
        scratch_shapes=[pltpu.SemaphoreType.DMA],
        compiler_params=PARAMS,
        cost_estimate=CHEAP,
    )(value, after)


def body(tokens, out_grads, basis_act, basis_grad):
    where = jnp.stack([lax.axis_index(axis) for axis in AXES]).astype(jnp.int32)
    joined, turned = prepare(tokens, out_grads)
    block = lax.ppermute(joined, AXES, permutation(to_group))
    (turned,) = in_order(block, turned)
    own = direct(turned, Y)
    near = gather_near(block, where, False, own[1:])
    stack = stack_up(where, own)
    stack, near = lax.optimization_barrier((stack, near))
    stacks = (stack, shifted(stack, ZL, 1))
    left, right = shifted(near, X, 1), shifted(near, X, -1)
    own = [near, left, right]
    far = relay(where, left, right)
    other = [shifted(piece, C, 1) for piece in own]
    *some, token = rotate_some(where, own + other, basis_act, basis_grad, stacks[1])
    last = [far, shifted(pass_on(far, token), C, 1)]
    panel = own + last[:1] + other + last[1:]
    *parts, act_kept, act_sent = rotate_last(where, last, basis_act, basis_grad, some)
    cov_act, cov_grad, done = covariance(where, panel, stacks)
    split, sq_act = act_squares(act_kept, act_sent)
    sq_grad = grad_squares(*sum_over_y(parts, where, (split,)))
    block = lax.ppermute(sq_act, AXES, permutation(to_group))
    pair = pair_up(sq_grad, where, 0)
    pair, block = lax.optimization_barrier((pair, block))
    squares_own = direct(pair, Y)
    squares = gather_far(gather_near(block, where, True, squares_own[1:3] + [done]))
    correction = correct(where, squares, squares_own)
    return (cov_act, cov_grad, correction)


def solution(mesh):
    fine = Mesh(mesh.devices.reshape(SIZES), AXES)
    dp, tensor = ("zl", "y"), ("x", "zh", "c")
    placed = P(dp, tensor)
    return jax.shard_map(
        body,
        mesh=fine,
        in_specs=(placed,) * 4,
        out_specs=(P(tensor, dp), P(tensor, dp), placed),
        check_vma=False,
    )
```

```python
import itertools

import jax
import jax.numpy as jnp
from jax import lax
from jax.experimental import pallas as pl
from jax.experimental.pallas import tpu as pltpu
from jax.sharding import Mesh, PartitionSpec as P

AXES = ("zl", "y", "x", "zh", "c")
SIZES = (2, 4, 4, 4, 2)
ZL, Y, X, ZH, C = range(5)
STEPS = (0, 1, -1, 2)
ANY = pl.BlockSpec(memory_space=pl.ANY)
WHOLE = pl.BlockSpec(memory_space=pltpu.VMEM)
SCALARS = pl.BlockSpec(memory_space=pltpu.SMEM)
PARAMS = pltpu.CompilerParams(vmem_limit_bytes=48 * 1024 * 1024)

CHEAP = pl.CostEstimate(flops=1000, bytes_accessed=1000, transcendentals=0)
LONG = pl.CostEstimate(flops=5 * 10**9, bytes_accessed=20 * 10**6, transcendentals=0)


def device_index(q):
    index = 0
    for size, value in zip(SIZES, q):
        index = index * size + value
    return index


def permutation(target):
    every = itertools.product(*(range(size) for size in SIZES))
    return [(device_index(q), device_index(target(*q))) for q in every]


def shifted(value, axis, step):
    def target(*q):
        q = list(q)
        q[axis] = (q[axis] + step) % SIZES[axis]
        return q

    return lax.ppermute(value, AXES, permutation(target))


def direct(value, axis):
    return [value if step == 0 else shifted(value, axis, step) for step in STEPS]


def folded(value):
    def target(zl, y, x, zh, c):
        return zl, y, (x - 1 + 2 * c) % SIZES[X], zh, c

    return lax.ppermute(value, AXES, permutation(target))


def to_group(zl, y, x, zh, c):
    row = (x & 1) * 2 + (zh >> 1)
    flip = zl ^ (x >> 1)
    return x >> 1, row, x ^ y ^ row, ((zh >> 1) ^ flip) * 2 + ((zh & 1) ^ flip), c


def x_slot(where, step):
    return ((where[X] - step) & 3) ^ (where[ZL] * 2 + (where[Y] >> 1)) ^ where[Y]


def y_slot(where, step):
    return (where[Y] - step) & 3


def z_slot(where, step):
    slot = (where[ZH] - step) & 3
    flip = (slot >> 1) ^ (where[Y] & 1)
    return flip ^ where[ZL], (slot & 1) ^ flip


def near_kernel(turned, where, *refs):
    pieces, near, sems = refs[:4], refs[-2], refs[-1]
    copies = []
    for i, (step, piece) in enumerate(zip(STEPS, pieces)):
        zl, h = z_slot(where, step)
        tokens = piece.shape[1 if turned else 0]
        span = pl.ds(pl.multiple_of(zl * tokens, tokens), tokens)
        target = near.at[h, :, span] if turned else near.at[h, span, :]
        copies.append(pltpu.make_async_copy(piece, target, sems.at[i]))
        copies[-1].start()
    for copy in copies:
        copy.wait()


def gather_near(block, where, turned, after):
    rows, columns = block.shape
    shape = (2, rows, 2 * columns) if turned else (2, 2 * rows, columns)
    return pl.pallas_call(
        lambda *refs: near_kernel(turned, *refs),
        out_shape=jax.ShapeDtypeStruct(shape, block.dtype),
        in_specs=[SCALARS] + [ANY] * (4 + len(after)),
        out_specs=ANY,
        scratch_shapes=[pltpu.SemaphoreType.DMA((4,))],
        compiler_params=PARAMS,
        cost_estimate=CHEAP,
    )(where, *direct(block, ZH), *after)


def stack_kernel(where, *refs):
    *pieces, stack, sems = refs
    copies = []
    for i, (step, piece) in enumerate(zip(STEPS, pieces)):
        copies.append(pltpu.make_async_copy(piece, stack.at[y_slot(where, step)], sems.at[i]))
        copies[-1].start()
    for copy in copies:
        copy.wait()


def stack_up(where, pieces):
    return pl.pallas_call(
        stack_kernel,
        out_shape=jax.ShapeDtypeStruct((4,) + pieces[0].shape, pieces[0].dtype),
        in_specs=[SCALARS] + [ANY] * 4,
        out_specs=ANY,
        scratch_shapes=[pltpu.SemaphoreType.DMA((4,))],
        compiler_params=PARAMS,
        cost_estimate=CHEAP,
    )(where, *pieces)


def gather_far(near):
    own = direct(near, X)
    return own + [shifted(piece, C, 1) for piece in own]


def relay(where, left, right):
    return folded(jnp.where(where[C] == 0, right, left))


def fetch(where, pieces, panel, sems):
    copies = []
    for i, step in enumerate(STEPS):
        for j in range(2):
            copies.append(
                pltpu.make_async_copy(
                    pieces[i + 4 * j],
                    panel.at[where[C] ^ j, x_slot(where, step)],
                    sems.at[i, j],
                )
            )
            copies[-1].start()
    return copies


def dot(a, b):
    return jnp.dot(a, b, preferred_element_type=jnp.float32)


def encode(value, out):
    rows, n = value.shape
    top = jnp.max(jnp.max(jnp.abs(value), axis=0, keepdims=True), axis=1, keepdims=True)
    top = jnp.maximum(top, 1e-30).astype(jnp.bfloat16)
    power = value * (32768.0 / top.astype(jnp.float32))
    sign = power < 0
    for _ in range(3):
        power = power * power
    out[:rows, :] = jnp.where(sign, -power, power).astype(jnp.bfloat16)
    out[rows:, :] = jnp.broadcast_to(top, (16, n))


def decode(coded):
    rows = coded.shape[0] - 16
    power = coded[:rows, :].astype(jnp.float32)
    top = coded[rows:rows + 1, :].astype(jnp.float32) * (1.0 / 32768.0)
    size = jnp.abs(power)
    root = lax.rsqrt(lax.rsqrt(size))
    root = jnp.where(size < 1.1754944e-38, 0.0, root * lax.rsqrt(root) * top)
    return jnp.where(power < 0, -root, root)


def product(panel, basis, low, k):
    total = None
    for h in range(2):
        for c in range(2):
            rows = basis[(2 * h + c) * k:(2 * h + c + 1) * k, :]
            term = dot(panel(h, c)[:, low:low + k], rows)
            total = term if total is None else total + term
    return total


def rotate_some_kernel(where, *refs):
    pieces, (act_ref, grad_ref) = refs[:6], refs[6:8]
    grad_full, grad_coded, act_kept, act_sent, token = refs[-11:-6]
    panel, act, grad, held, in_sems, basis_sems = refs[-6:]
    token[...] = jnp.zeros_like(token)
    n = act.shape[1]
    copies = [
        pltpu.make_async_copy(act_ref, act, basis_sems.at[0]),
        pltpu.make_async_copy(grad_ref, grad, basis_sems.at[1]),
    ]
    for i in range(3):
        for j in range(2):
            copies.append(
                pltpu.make_async_copy(
                    pieces[i + 3 * j], panel.at[where[C] ^ j, i], in_sems.at[i, j]
                )
            )
    for copy in copies:
        copy.start()
    for copy in copies:
        copy.wait()
    rows = act_kept.shape[1]
    for i in range(3):
        total = product(lambda h, c: panel[c, i, h], grad, n, 2 * n)
        grad_full[i] = total
        encode(total, grad_coded.at[i])
        total = product(lambda h, c: panel[c, i, h], act, 0, n)
        held[0] = total[:rows]
        held[1] = total[rows:]
        act_kept[i] = held[where[ZL]]
        encode(held[1 - where[ZL]], act_sent.at[i])


def rotate_some(where, pieces, basis_act, basis_grad, after):
    rows, k = pieces[0].shape[1:]
    n = k // 3
    f32, bf16 = jnp.float32, jnp.bfloat16
    return pl.pallas_call(
        rotate_some_kernel,
        out_shape=[
            jax.ShapeDtypeStruct((3, rows, 2 * n), f32),
            jax.ShapeDtypeStruct((3, rows + 16, 2 * n), bf16),
            jax.ShapeDtypeStruct((3, rows // 2, n), f32),
            jax.ShapeDtypeStruct((3, rows // 2 + 16, n), bf16),
            jax.ShapeDtypeStruct((8, 128), f32),
        ],
        in_specs=[SCALARS] + [ANY] * 9,
        scratch_shapes=[
            pltpu.VMEM((2, 3, 2, rows, k), bf16),
            pltpu.VMEM(basis_act.shape, bf16),
            pltpu.VMEM(basis_grad.shape, bf16),
            pltpu.VMEM((2, rows // 2, n), f32),
            pltpu.SemaphoreType.DMA((3, 2)),
            pltpu.SemaphoreType.DMA((2,)),
        ],
        compiler_params=PARAMS,
        cost_estimate=LONG,
    )(where, *pieces, basis_act, basis_grad, after)


def rotate_last_kernel(where, *refs):
    pieces, (act_ref, grad_ref), done = refs[:2], refs[2:4], refs[4:8]
    outs, act_kept, act_sent = refs[8:12], refs[12], refs[13]
    panel, act, grad, held, grad_full, grad_coded, kept, sent, in_sems, out_sems = refs[14:]
    n = act.shape[1]
    copies = [
        pltpu.make_async_copy(act_ref, act, in_sems.at[0]),
        pltpu.make_async_copy(grad_ref, grad, in_sems.at[1]),
    ]
    for j in range(2):
        copies.append(
            pltpu.make_async_copy(pieces[j], panel.at[where[C] ^ j], in_sems.at[2 + j])
        )
    for copy in copies:
        copy.start()

    def route(i, step, sources, act_on):
        due = (x_slot(where, step) - where[Y]) & 3
        for j, y_step in enumerate(STEPS):
            @pl.when(due == (y_step & 3))
            def _():
                source = sources[0] if j == 0 else sources[1]
                for copy in (
                    pltpu.make_async_copy(source, outs[j], out_sems.at[i, 0]),
                    pltpu.make_async_copy(sources[2], act_kept.at[j], out_sems.at[i, 1]),
                    pltpu.make_async_copy(sources[3], act_sent.at[j], out_sems.at[i, 2]),
                ):
                    act_on(copy)

    parts = [(i, STEPS[i], [ref.at[i] for ref in done]) for i in range(3)]
    for part in parts:
        route(*part, lambda copy: copy.start())
    for copy in copies:
        copy.wait()
    rows = kept.shape[0]
    total = product(lambda h, c: panel[c, h], grad, n, 2 * n)
    grad_full[...] = total
    encode(total, grad_coded)
    total = product(lambda h, c: panel[c, h], act, 0, n)
    held[0] = total[:rows]
    held[1] = total[rows:]
    kept[...] = held[where[ZL]]
    encode(held[1 - where[ZL]], sent)
    parts.append((3, STEPS[3], [grad_full, grad_coded, kept, sent]))
    route(*parts[3], lambda copy: copy.start())
    for part in parts:
        route(*part, lambda copy: copy.wait())


def rotate_last(where, pieces, basis_act, basis_grad, done):
    rows, k = pieces[0].shape[1:]
    n = k // 3
    f32, bf16 = jnp.float32, jnp.bfloat16
    return pl.pallas_call(
        rotate_last_kernel,
        out_shape=[jax.ShapeDtypeStruct((rows, 2 * n), f32)]
        + [jax.ShapeDtypeStruct((rows + 16, 2 * n), bf16)] * 3
        + [
            jax.ShapeDtypeStruct((4, rows // 2, n), f32),
            jax.ShapeDtypeStruct((4, rows // 2 + 16, n), bf16),
        ],
        in_specs=[SCALARS] + [ANY] * 8,
        out_specs=[ANY] * 6,
        scratch_shapes=[
            pltpu.VMEM((2, 2, rows, k), bf16),
            pltpu.VMEM(basis_act.shape, bf16),
            pltpu.VMEM(basis_grad.shape, bf16),
            pltpu.VMEM((2, rows // 2, n), f32),
            pltpu.VMEM((rows, 2 * n), f32),
            pltpu.VMEM((rows + 16, 2 * n), bf16),
            pltpu.VMEM((rows // 2, n), f32),
            pltpu.VMEM((rows // 2 + 16, n), bf16),
            pltpu.SemaphoreType.DMA((4,)),
            pltpu.SemaphoreType.DMA((4, 3)),
        ],
        compiler_params=PARAMS,
        cost_estimate=CHEAP,
    )(where, *pieces, basis_act, basis_grad, *done)


def covariance_kernel(where, *refs):
    pieces, stacks, outs, token = refs[:8], refs[8:10], refs[10:12], refs[12]
    panel, own, act, grad, in_sems, own_sems, out_sems = refs[13:]
    token[...] = jnp.zeros_like(token)
    n = act.shape[1]
    rows = stacks[0].shape[2]
    tokens = 2 * rows
    copies = []
    for i, stack in enumerate(stacks):
        for y in range(4):
            start = pl.multiple_of((2 * y + (where[ZL] ^ i)) * rows, rows)
            copies.append(
                pltpu.make_async_copy(stack.at[y], own.at[:, pl.ds(start, rows)], own_sems.at[i, y])
            )
            copies[-1].start()
    copies += fetch(where, pieces, panel, in_sems)
    for copy in copies:
        copy.wait()
    scale = 1.0 / (4 * tokens)
    waits = []
    for h in range(2):
        for c in range(2):
            block = 2 * h + c
            for j, (held, out, low, k) in enumerate(((act, outs[0], 0, n), (grad, outs[1], n, 2 * n))):
                total = None
                for y in range(4):
                    term = dot(
                        own[low:low + k, y * tokens:(y + 1) * tokens],
                        panel[c, y, h, :, low:low + k],
                    )
                    total = term if total is None else total + term
                held[block] = total * scale
                waits.append(
                    pltpu.make_async_copy(
                        held.at[block], out.at[:, block * k:(block + 1) * k], out_sems.at[block, j]
                    )
                )
                waits[-1].start()
    for copy in waits:
        copy.wait()


def covariance(where, pieces, mine):
    rows, k = pieces[0].shape[1:]
    n = k // 3
    f32, bf16 = jnp.float32, jnp.bfloat16
    return pl.pallas_call(
        covariance_kernel,
        out_shape=[
            jax.ShapeDtypeStruct((n, 4 * n), f32),
            jax.ShapeDtypeStruct((2 * n, 8 * n), f32),
            jax.ShapeDtypeStruct((8, 128), f32),
        ],
        in_specs=[SCALARS] + [ANY] * 10,
        out_specs=[ANY] * 2 + [WHOLE],
        scratch_shapes=[
            pltpu.VMEM((2, 4, 2, rows, k), bf16),
            pltpu.VMEM((k, 4 * rows), bf16),
            pltpu.VMEM((4, n, n), f32),
            pltpu.VMEM((4, 2 * n, 2 * n), f32),
            pltpu.SemaphoreType.DMA((4, 2)),
            pltpu.SemaphoreType.DMA((2, 4)),
            pltpu.SemaphoreType.DMA((4, 2)),
        ],
        compiler_params=PARAMS,
        cost_estimate=LONG,
    )(where, *pieces, *mine)


def correction_kernel(where, *refs):
    pieces, squares, out = refs[:8], refs[8:12], refs[12]
    panel, grad, held, in_sems, grad_sems, out_sems = refs[13:]
    rows, tokens = panel.shape[3:]
    copies = fetch(where, pieces, panel, in_sems)
    for i, step in enumerate(STEPS):
        copies.append(
            pltpu.make_async_copy(squares[i], grad.at[y_slot(where, step)], grad_sems.at[i])
        )
        copies[-1].start()
    for copy in copies:
        copy.wait()
    scale = 1.0 / (4 * tokens)
    waits = []
    for h in range(2):
        for c in range(2):
            block = 2 * h + c
            total = None
            for y in range(4):
                term = dot(panel[c, y, h], grad[y])
                total = term if total is None else total + term
            held[block] = total * scale
            waits.append(
                pltpu.make_async_copy(
                    held.at[block], out.at[block * rows:(block + 1) * rows, :], out_sems.at[block]
                )
            )
            waits[-1].start()
    for copy in waits:
        copy.wait()


def correct(where, pieces, squares):
    rows, tokens = pieces[0].shape[1:]
    n = squares[0].shape[1]
    f32, bf16 = jnp.float32, jnp.bfloat16
    return pl.pallas_call(
        correction_kernel,
        out_shape=jax.ShapeDtypeStruct((4 * rows, n), f32),
        in_specs=[SCALARS] + [ANY] * 12,
        out_specs=ANY,
        scratch_shapes=[
            pltpu.VMEM((2, 4, 2, rows, tokens), bf16),
            pltpu.VMEM((4, tokens, n), bf16),
            pltpu.VMEM((4, rows, n), f32),
            pltpu.SemaphoreType.DMA((4, 2)),
            pltpu.SemaphoreType.DMA((4,)),
            pltpu.SemaphoreType.DMA((4,)),
        ],
        compiler_params=PARAMS,
        cost_estimate=CHEAP,
    )(where, *pieces, *squares)


def half_kernel(where, own, *refs):
    arrived, kept, sent, total = refs[:3], refs[-3], refs[-2], refs[-1]
    rows = kept.shape[0]
    whole = own[...]
    for coded in arrived:
        whole = whole + decode(coded)
    for i in range(2):
        total[i] = whole[i * rows:(i + 1) * rows]
    kept[...] = total[where[ZL]]
    encode(total[1 - where[ZL]], sent)


def sum_over_y(parts, where, after=()):
    rows, n = parts[0].shape
    rows = rows // 2
    parts = [part if step == 0 else shifted(part, Y, step) for step, part in zip(STEPS, parts)]
    return pl.pallas_call(
        half_kernel,
        out_shape=[
            jax.ShapeDtypeStruct((rows, n), jnp.float32),
            jax.ShapeDtypeStruct((rows + 16, n), jnp.bfloat16),
        ],
        in_specs=[SCALARS] + [WHOLE] * 4 + [ANY] * len(after),
        scratch_shapes=[pltpu.VMEM((2, rows, n), jnp.float32)],
        compiler_params=PARAMS,
        cost_estimate=CHEAP,
    )(where, *parts, *after)


def grad_square_kernel(kept, arrived, out):
    total = kept[...] + decode(arrived)
    out[...] = (total * total).astype(jnp.bfloat16)


def grad_squares(kept, sent):
    return pl.pallas_call(
        grad_square_kernel,
        out_shape=jax.ShapeDtypeStruct(kept.shape, jnp.bfloat16),
        compiler_params=PARAMS,
        cost_estimate=CHEAP,
    )(kept, shifted(sent, ZL, 1))


def split_kernel(kept, arrived, *outs):
    rows, n = kept.shape[1:]
    outs[0][...] = kept[0] + decode(arrived.at[0])
    for i in range(1, 4):
        encode(kept[i] + decode(arrived.at[i]), outs[i])


def act_square_kernel(own, *refs):
    total = own[...]
    for coded in refs[:3]:
        total = total + decode(coded)
    refs[3][...] = (total * total).T.astype(jnp.bfloat16)


def act_squares(kept, sent):
    rows, n = kept.shape[1:]
    parts = pl.pallas_call(
        split_kernel,
        out_shape=[jax.ShapeDtypeStruct((rows, n), jnp.float32)]
        + [jax.ShapeDtypeStruct((rows + 16, n), jnp.bfloat16)] * 3,
        compiler_params=PARAMS,
        cost_estimate=CHEAP,
    )(kept, shifted(sent, ZL, 1))
    return parts[0], pl.pallas_call(
        act_square_kernel,
        out_shape=jax.ShapeDtypeStruct((n, rows), jnp.bfloat16),
        compiler_params=PARAMS,
        cost_estimate=CHEAP,
    )(*[part if step == 0 else shifted(part, Y, step) for step, part in zip(STEPS, parts)])


def pair_kernel(axis, where, own, other, pair, sems):
    size = own.shape[axis]
    copies = []
    for i, (ref, zl) in enumerate(((own, where[ZL]), (other, 1 - where[ZL]))):
        span = pl.ds(pl.multiple_of(zl * size, size), size)
        target = pair.at[:, span] if axis else pair.at[span, :]
        copies.append(pltpu.make_async_copy(ref, target, sems.at[i]))
        copies[-1].start()
    for copy in copies:
        copy.wait()


def pair_up(block, where, axis):
    shape = list(block.shape)
    shape[axis] *= 2
    return pl.pallas_call(
        lambda *refs: pair_kernel(axis, *refs),
        out_shape=jax.ShapeDtypeStruct(shape, block.dtype),
        in_specs=[SCALARS] + [ANY] * 2,
        out_specs=ANY,
        scratch_shapes=[pltpu.SemaphoreType.DMA((2,))],
        compiler_params=PARAMS,
        cost_estimate=CHEAP,
    )(where, block, shifted(block, ZL, 1))


def prepare_kernel(tokens, out_grads, joined, turned):
    n = tokens.shape[1]
    joined[:, :n] = tokens[...]
    joined[:, n:] = out_grads[...]
    turned[:n, :] = tokens[...].T
    turned[n:, :] = out_grads[...].T


def prepare(tokens, out_grads):
    rows, k = tokens.shape[0], tokens.shape[1] + out_grads.shape[1]
    return pl.pallas_call(
        prepare_kernel,
        out_shape=[
            jax.ShapeDtypeStruct((rows, k), tokens.dtype),
            jax.ShapeDtypeStruct((k, rows), tokens.dtype),
        ],
        compiler_params=PARAMS,
        cost_estimate=CHEAP,
    )(tokens, out_grads)


def in_order(first, *later):
    return lax.optimization_barrier((first, *later))[1:]


def pass_kernel(value, after, out, sem):
    copy = pltpu.make_async_copy(value, out, sem)
    copy.start()
    copy.wait()


def pass_on(value, after):
    return pl.pallas_call(
        pass_kernel,
        out_shape=jax.ShapeDtypeStruct(value.shape, value.dtype),
        in_specs=[ANY] * 2,
        out_specs=ANY,
        scratch_shapes=[pltpu.SemaphoreType.DMA],
        compiler_params=PARAMS,
        cost_estimate=CHEAP,
    )(value, after)


def body(tokens, out_grads, basis_act, basis_grad):
    where = jnp.stack([lax.axis_index(axis) for axis in AXES]).astype(jnp.int32)
    joined, turned = prepare(tokens, out_grads)
    block = lax.ppermute(joined, AXES, permutation(to_group))
    (turned,) = in_order(block, turned)
    own = direct(turned, Y)
    near = gather_near(block, where, False, own[1:])
    stack = stack_up(where, own)
    stack, near = lax.optimization_barrier((stack, near))
    stacks = (stack, shifted(stack, ZL, 1))
    left, right = shifted(near, X, 1), shifted(near, X, -1)
    own = [near, left, right]
    far = relay(where, left, right)
    other = [shifted(piece, C, 1) for piece in own]
    *some, token = rotate_some(where, own + other, basis_act, basis_grad, stacks[1])
    last = [far, shifted(pass_on(far, token), C, 1)]
    panel = own + last[:1] + other + last[1:]
    *parts, act_kept, act_sent = rotate_last(where, last, basis_act, basis_grad, some)
    cov_act, cov_grad, done = covariance(where, panel, stacks)
    split, sq_act = act_squares(act_kept, act_sent)
    sq_grad = grad_squares(*sum_over_y(parts, where, (split,)))
    block = lax.ppermute(sq_act, AXES, permutation(to_group))
    pair = pair_up(sq_grad, where, 0)
    pair, block = lax.optimization_barrier((pair, block))
    squares_own = direct(pair, Y)
    squares = gather_far(gather_near(block, where, True, squares_own[1:3] + [done]))
    correction = correct(where, squares, squares_own)
    return (cov_act, cov_grad, correction)


def solution(mesh):
    fine = Mesh(mesh.devices.reshape(SIZES), AXES)
    dp, tensor = ("zl", "y"), ("x", "zh", "c")
    placed = P(dp, tensor)
    return jax.shard_map(
        body,
        mesh=fine,
        in_specs=(placed,) * 4,
        out_specs=(P(tensor, dp), P(tensor, dp), placed),
        check_vma=False,
    )
```
